512 devices in a mesh: kv: 128 (over x, z, core), pair: 4 (over y).
Axes of the slice: x: 4, y: 4, z: 16, core: 2. Of those that a mesh axis runs over, the one named last changes fastest.
Arguments:
- query: bfloat16 [16, 8192], P(None, ('kv', 'pair')), may hold values from -27 to 27
- key_cache: bfloat16 [16, 16384, 512], P(None, ('kv', 'pair')), may hold values from -9 to 9
- value_cache: bfloat16 [16, 16384, 512], P(None, ('kv', 'pair')), may hold values from -6 to 6
- lengths: int32 [16], replicated, may hold values from 2049 to 16384, as said below
- hidden_in: bfloat16 [16, 4096], P(None, ('kv', 'pair')), may hold values from -40 to 40
- out_proj: bfloat16 [8192, 4096], P(('kv', 'pair')), may hold values from -0.25 to 0.25
- norm_gain: bfloat16 [4096], replicated, may hold values from 0.099609375 to 1.8984375
- expert_ids: int32 [16, 8], replicated, may hold values from 0 to 63, all different within a row; in each aligned block of 16 rows (0 to 15, 16 to 31, ...) at most 4 rows name the same one
- route_weights: float32 [16, 8], replicated, may hold values from 0.1 to 1
- w_gate: bfloat16 [65536, 4096], P(('kv', 'pair')), may hold values from -0.09375 to 0.09375
- w_up: bfloat16 [65536, 4096], P(('kv', 'pair')), may hold values from -0.09375 to 0.09375
- w_down: bfloat16 [65536, 4096], P(('kv', 'pair')), may hold values from -0.75 to 0.75
Outputs:
- context: bfloat16 [16, 8192], P(None, ('kv', 'pair'))
- layer_out: bfloat16 [16, 4096], P(None, ('kv', 'pair'))
The draws below stay inside these ranges and needn't reach their ends.
Inputs may be any that keep to these rules, and one draw needn't show every extreme that they name: `lengths`: every sequence uses its first positions; some sequence uses all 16384. `expert_ids`: each row names 8 different experts; every expert is named by some row, none by more than 4 rows, and one by exactly 4.
All inputs are finite; a program needn't handle non-finite values.
Results may differ from the reference program's by a relative error of at most 0.01155.
Values may be sent and summed in bfloat16 or wider, within the bound.
No kernel may reach another device: no remote copies, remote signals or barrier semaphores. Data moves between devices by JAX's collectives and lax.ppermute only.
A program may use at most 64 MiB of HBM per device.

```python
import math
import jax
import jax.numpy as jnp
import numpy as np
from jax import lax

D = 4096
H = 64
KVH = 4
HD = 128
FE = 1024
TOPK = 8
B = 16
EXPERTS = 64
L = 16384
MOST = 4


def draw_query(key, part):
    key = jax.random.fold_in(key, 3)
    result = jnp.clip(2.5 * jax.random.normal(key, (B, H, HD), jnp.float32), -10.0, 10.0)
    return result.reshape(B, H * HD).astype(jnp.bfloat16)


def draw_key_cache(key, part):
    key = jax.random.fold_in(key, 5)
    result = jnp.clip(jax.random.normal(key, (B, L, KVH * HD), jnp.float32), -6.0, 6.0)
    return result.astype(jnp.bfloat16)


def draw_lengths(key, part):
    key = jax.random.fold_in(key, 7)
    first_key, second_key = jax.random.split(key)
    drawn = jax.random.randint(first_key, (B,), L // 8 + 1, L + 1)
    longest = jax.random.randint(second_key, (), 0, B)
    return jnp.where(jnp.arange(B) == longest, L, drawn).astype(jnp.int32)


def draw_hidden_in(key, part):
    key = jax.random.fold_in(key, 9)
    row_key, column_key, noise_key = jax.random.split(key, 3)
    columns = jnp.exp(jax.random.uniform(column_key, (1, D), jnp.float32, math.log(0.3), math.log(3.0)))
    rows = jnp.exp(jax.random.uniform(row_key, (B, 1), jnp.float32, math.log(0.3), math.log(3.0)))
    noise = jnp.clip(jax.random.normal(noise_key, (B, D), jnp.float32), -4.0, 4.0)
    result = noise * rows * columns
    return jnp.clip(result, -40.0, 40.0).astype(jnp.bfloat16)


def spiked(values, rng, source, target, shards_of, factor):
    owner, partner = [(jnp.arange(values.shape[position]) // (values.shape[position] // shards_of)).reshape([-1 if axis == position else 1 for axis in range(values.ndim)]) for position in (source, target)]
    chosen = jax.random.permutation(rng, shards_of)[partner]
    strong = (owner == chosen) | (owner == (partner + shards_of // 2) % shards_of)
    return jnp.where(strong, factor * values, values)


def block_levels(key, shape, shards, least, high):
    level = 1.0
    for position, shards_of in shards:
        draws = jax.random.uniform(jax.random.fold_in(jax.random.fold_in(key, 6), position), (shards_of,), jnp.float32, least / len(shards), high / len(shards))
        level = level * jnp.repeat(jnp.exp(draws), shape[position] // shards_of).reshape((-1,) + (1,) * (len(shape) - 1 - position))
    return level


def routed_block(own_key, own, number, rows, count, top, limit, skew):
    order = jax.random.permutation(own_key, count)
    packed, usual = portions_of(count, rows * top, limit, skew, True), portions_of(count, rows * top, limit, skew, False)
    places = jnp.arange(count)

    def named(sizes, turn):
        used = int((sizes > 0).sum())
        fixed = max(1, used // 4)
        shifted = fixed + (places - fixed + turn * (used - fixed)) % max(1, count - fixed)
        return jnp.zeros((count,), jnp.int32).at[order[jnp.where(places < fixed, places, shifted)]].set(jnp.asarray(sizes, jnp.int32))

    sizes = jnp.where(number % 4 == 0, named(packed, number // 4), named(usual, number - number // 4 - 1))
    mixed = jax.random.permutation(jax.random.fold_in(own, 3), count)
    source_of, sink = mixed[0:count // 2 * 2:2], mixed[1:count // 2 * 2:2]
    margin = jnp.minimum(sizes[source_of] - 1, limit - sizes[sink]) // 2
    margin = jnp.where((source_of == order[0]) | (sink == order[0]) | (sizes[sink] == 0), 0, jnp.maximum(margin, 0))
    shifted = jax.random.randint(jax.random.fold_in(own, 4), (count // 2,), 0, 1 << 20) % (margin + 1)
    sizes = sizes.at[source_of].add(-shifted).at[sink].add(shifted)
    labels = jnp.searchsorted(jnp.cumsum(sizes), jnp.arange(rows * top), side="right").astype(jnp.int32)
    grid = labels.reshape(top, rows).T
    grid = grid[jax.random.permutation(jax.random.fold_in(own, 1), rows)]
    turn = jax.random.randint(jax.random.fold_in(own, 2), (rows, 1), 0, top)
    return jnp.take_along_axis(grid, (jnp.arange(top)[None, :] + turn) % top, axis=1)


def portions_of(count, total, bound, slope, full):
    weights = [(1 << 20) // math.isqrt(rank ** slope) + 1 for rank in range(1, count + 1)]
    largest = bound if full else min(bound, max(-(-total // count), total * weights[0] // sum(weights)))
    least = 1 if total - largest >= count - 1 else 0
    holding, spare = [largest] + [least] * (count - 1), total - largest - least * (count - 1)
    while spare > 0:
        candidates = [i for i in range(1, count) if holding[i] < largest] or [i for i in range(1, count) if holding[i] < bound]
        pool, budget = sum([weights[i] for i in candidates]), spare
        for i in candidates:
            extra = min(bound - holding[i], max(1, budget * weights[i] // pool), spare)
            holding[i] = holding[i] + extra
            spare = spare - extra
    return np.array(holding)


def gaussian(key, dims, scale, bound, cuts=(), kind=jnp.bfloat16):
    values = scale * jax.random.normal(key, dims, jnp.float32)
    if cuts:
        values = values * block_levels(key, dims, cuts, -0.22, 0.18)
    return jnp.clip(values, -bound, bound).astype(kind)


def noise_with(rng, shape, scale, limit, shards, heavy, kind=jnp.bfloat16):
    values = scale * jax.random.normal(rng, shape, jnp.float32)
    if shards:
        values = values * block_levels(rng, shape, shards, -0.22, 0.18)
    return jnp.clip(spiked(values, jax.random.fold_in(rng, 3), *heavy), -limit, limit).astype(kind)


def setup_inputs(seed: int = 0) -> dict:
    streams_of = jax.random.split(jax.random.key(seed), 13)
    query = draw_query(jax.random.fold_in(streams_of[12], 71), 0)
    key_cache = draw_key_cache(jax.random.fold_in(streams_of[12], 71), 0)
    value_cache = gaussian(streams_of[2], (B, L, KVH * HD), 1.0, 6.0, ((1, 512),))
    lengths = draw_lengths(jax.random.fold_in(streams_of[12], 71), 0)
    hidden_in = draw_hidden_in(jax.random.fold_in(streams_of[12], 71), 0)
    out_proj = noise_with(streams_of[5], (H * HD, D), (H * HD) ** -0.5, 0.25, ((0, 512),), (0, 1, 512, 6.0))
    norm_gain = jnp.clip(1.0 + 0.18 * jax.random.normal(streams_of[6], (D,), jnp.float32), 0.099609375, 1.8984375).astype(jnp.bfloat16)
    expert_ids_keys = jax.random.split(jax.random.fold_in(streams_of[7], 1), B // B)
    expert_ids_turns = jax.random.permutation(jax.random.fold_in(streams_of[7], 3), B // B)
    expert_ids = jax.vmap(lambda own, number: routed_block(jax.random.fold_in(streams_of[7], 2), own, number, B, EXPERTS, TOPK, MOST, 0))(expert_ids_keys, expert_ids_turns).reshape((B, TOPK))
    route_weights = jnp.clip(jnp.exp(jax.random.uniform(streams_of[8], (B, TOPK), jnp.float32, math.log(0.1), math.log(1.0))), 0.1, 1.0)
    w_gate = gaussian(streams_of[9], (EXPERTS * FE, D), D ** -0.5, 0.09375, ((0, 512),))
    w_up = gaussian(streams_of[10], (EXPERTS * FE, D), D ** -0.5, 0.09375, ((0, 512),))
    w_down = noise_with(streams_of[11], (EXPERTS * FE, D), FE ** -0.5, 0.75, ((0, 512),), (0, 1, 512, 6.0))
    return {"query": query, "key_cache": key_cache, "value_cache": value_cache, "lengths": lengths, "hidden_in": hidden_in, "out_proj": out_proj, "norm_gain": norm_gain, "expert_ids": expert_ids, "route_weights": route_weights, "w_gate": w_gate, "w_up": w_up, "w_down": w_down}


floor_score = -1e+30

def slot_tables(expert_ids, share, count, slot_count):
    experts = jnp.arange(count, dtype=jnp.int32)
    match = expert_ids[None, :, :] == experts[:, None, None]
    hits = lax.optimization_barrier(jnp.sum(match.astype(jnp.int32), axis=2))
    weight = lax.optimization_barrier(jnp.sum(jnp.where(match, share[None, :, :], 0.0), axis=2))
    order = jnp.cumsum(hits, axis=1) - hits
    slots = jnp.arange(slot_count, dtype=jnp.int32)
    table = ((hits[:, None, :] == 1) & (order[:, None, :] == slots[None, :, None])).astype(jnp.float32)
    coefficient = lax.optimization_barrier(jnp.sum(table * weight[:, None, :], axis=2))
    return (table, coefficient)

def reference(query, key_cache, value_cache, lengths, hidden_in, out_proj, norm_gain, expert_ids, route_weights, w_gate, w_up, w_down):
    group = H // KVH
    queries = query.astype(jnp.float32).reshape(B, KVH, group, HD)
    keys = key_cache.astype(jnp.float32).reshape(B, L, KVH, HD)
    values = value_cache.astype(jnp.float32).reshape(B, L, KVH, HD)
    scores = jnp.einsum('bgqd,btgd->bgqt', queries, keys) / math.sqrt(HD)
    places = jnp.arange(L, dtype=jnp.int32)
    valid = (places[None, :] < lengths[:, None])[:, None, None, :]
    scores = jnp.where(valid, scores, floor_score)
    highest = lax.optimization_barrier(jnp.max(scores, axis=-1, keepdims=True))
    weights = jnp.where(valid, jnp.exp(scores - highest), 0.0)
    weights = weights / lax.optimization_barrier(jnp.sum(weights, axis=-1, keepdims=True))
    mixed = jnp.einsum('bgqt,btgd->bgqd', weights, values, precision=lax.Precision.HIGHEST)
    context = mixed.reshape(B, H * HD).astype(jnp.bfloat16)
    projected = jnp.dot(context, out_proj, preferred_element_type=jnp.float32)
    mid = (hidden_in.astype(jnp.float32) + projected).astype(jnp.bfloat16)
    mid_float = mid.astype(jnp.float32)
    scale = lax.rsqrt(lax.optimization_barrier(jnp.mean(mid_float * mid_float, axis=-1, keepdims=True)) + 1e-06)
    normed = (mid_float * scale * norm_gain.astype(jnp.float32)[None, :]).astype(jnp.bfloat16)
    share = route_weights / lax.optimization_barrier(jnp.sum(route_weights, axis=-1, keepdims=True))
    table, coefficient = slot_tables(expert_ids, share, EXPERTS, MOST)
    normed_float = normed.astype(jnp.float32)
    gate_all = w_gate.reshape(EXPERTS, FE, D)
    up_all = w_up.reshape(EXPERTS, FE, D)
    down_all = w_down.reshape(EXPERTS, FE, D)

    def expert_step(total, inputs):
        rows, coef_rows, gate_weight, up_weight, down_weight = inputs
        picked = jnp.dot(rows, normed_float, precision=lax.Precision.HIGHEST).astype(jnp.bfloat16)
        gate = jnp.dot(picked, gate_weight.T, preferred_element_type=jnp.float32)
        upward = jnp.dot(picked, up_weight.T, preferred_element_type=jnp.float32)
        hidden_units = (jax.nn.silu(gate) * upward).astype(jnp.bfloat16)
        weighted = jnp.dot(hidden_units, down_weight, preferred_element_type=jnp.float32) * coef_rows[:, None]
        return (total + jnp.dot(rows.T, weighted, precision=lax.Precision.HIGHEST), None)
    start_total = jnp.zeros((B, D), jnp.float32)
    mixture, _ = lax.scan(expert_step, start_total, (table, coefficient, gate_all, up_all, down_all))
    layer_out = (mid_float + mixture).astype(jnp.bfloat16)
    return (context, layer_out)
```

```python
import math

import jax
import jax.numpy as jnp
import numpy as np
from jax import lax
from jax.experimental import pallas as pl
from jax.experimental.pallas import tpu as pltpu
from jax.sharding import Mesh
from jax.sharding import PartitionSpec as P

HD = 128
X, Z, CY = 4, 16, 8
PLANE = X * CY
B = 16
D = 4096
SPAN = 32
FLOOR = -1e30
BF = jnp.bfloat16
F32 = jnp.float32
PLANE_AXES = ("x", "c", "y")
ALL_AXES = ("x", "z", "c", "y")


def iota(shape, dimension):
    return lax.broadcasted_iota(jnp.int32, shape, dimension)


def dot(a, b, dims, precision=None):
    return lax.dot_general(
        a, b, (dims, ((), ())), preferred_element_type=F32, precision=precision
    )


def eye(n, dtype=BF):
    return (iota((n, n), 0) == iota((n, n), 1)).astype(dtype)


def spread_query(arrived, out):
    rows = arrived[...].astype(F32).reshape(Z * 8, 48).astype(BF)
    turned = dot(rows, eye(Z * 8), ((0,), (0,))).astype(BF)
    for k in range(PLANE):
        out[k] = turned


def attend(place, lengths, gathered, keys, values, out, hidden_block):
    device = place[0]
    x, cy = place[1], place[3]
    lane_j = iota((SPAN, 128), 1) % 8
    position = device * SPAN + iota((SPAN, 128), 0)
    zeros = jnp.zeros((10, 128), F32)
    valids = []
    for i in range(2):
        valids.append(
            jnp.concatenate(
                [
                    ((lane_j == j) & (position < lengths[i * 8 + j])).astype(F32)
                    for j in range(8)
                ],
                axis=0,
            )
        )
    for g in range(X):
        stats = [[], [], []]
        for i in range(2):
            query = gathered[g * CY : (g + 1) * CY, i * 16 : (i + 1) * 16, :].reshape(HD, 128)
            k = keys[i * 8 : (i + 1) * 8, :, g * HD : (g + 1) * HD].reshape(8 * SPAN, HD)
            v = values[i * 8 : (i + 1) * 8, :, g * HD : (g + 1) * HD].reshape(8 * SPAN, HD)
            scores = dot(k, query, ((1,), (0,))) * (1.0 / math.sqrt(HD))
            valid = valids[i] > 0.5
            scores = jnp.where(valid, scores, FLOOR)
            top = jnp.max(scores, axis=0, keepdims=True).astype(BF).astype(F32)
            weights = jnp.where(valid, jnp.exp(scores - top), 0.0).astype(BF)
            total = jnp.sum(weights.astype(F32), axis=0, keepdims=True)
            mixed = dot(v, weights, ((0,), (0,))).astype(BF)
            for c in range(CY):
                out[g * CY + c, i * 16 : (i + 1) * 16, :] = mixed[c * 16 : (c + 1) * 16]
            high = total.astype(BF).astype(F32)
            stats[0].append(top)
            stats[1].append(high)
            stats[2].append(total - high)
        block = jnp.concatenate(stats[0] + stats[1] + stats[2] + [zeros], axis=0).astype(BF)
        for c in range(CY):
            out[g * CY + c, 32:48, :] = block
    own = gathered[pl.ds(x * CY, CY), 32:48, :]
    row, lane = iota((128, 128), 0), iota((128, 128), 1)
    pick = (row % 8 == lane % 8) & (row // 8 == 2 * cy + lane // 64)
    total = jnp.zeros((B, 128), F32)
    for c in range(CY):
        select = (pick & (lane // 8 % 8 == c)).astype(BF)
        total += dot(own[c], select, ((1,), (0,)))
    hidden_block[...] = total


def merge_plane(arrived, out):
    parts = []
    tops, highs, lows = [], [], []
    for i in range(2):
        top = arrived[:, 32 + i, :].astype(F32)
        total = arrived[:, 34 + i, :].astype(F32) + arrived[:, 36 + i, :].astype(F32)
        best = jnp.max(top, axis=0, keepdims=True)
        scale = jnp.exp(top - best)
        mass = jnp.sum(total * scale, axis=0, keepdims=True)
        mixed = arrived[:, i * 16 : (i + 1) * 16, :].astype(F32)
        parts.append(jnp.sum(mixed * scale[:, None, :], axis=0))
        high = mass.astype(BF).astype(F32)
        tops.append(best)
        highs.append(high)
        lows.append(mass - high)
    full = jnp.concatenate(
        parts + tops + highs + lows + [jnp.zeros((10, 128), F32)], axis=0
    ).astype(BF)
    turned = dot(eye(128), full, ((1,), (1,)))
    out[...] = turned.reshape(Z, 8, 48).astype(BF)


def finish_context(arrived, out_proj, context, out):
    rows = arrived[...].astype(F32).reshape(Z * 8, 48).astype(BF)
    row, lane = iota((48, 32), 0), iota((48, 32), 1)
    mixed = dot(rows, (row == lane).astype(BF), ((1,), (0,))).reshape(Z, 8, 32)
    top = dot(rows, (row == 32 + lane // 16).astype(BF), ((1,), (0,))).reshape(Z, 8, 32)
    both = (row == 34 + lane // 16) | (row == 36 + lane // 16)
    total = dot(rows, both.astype(BF), ((1,), (0,))).reshape(Z, 8, 32)
    scale = jnp.exp(top - jnp.max(top, axis=0, keepdims=True))
    done = jnp.sum(mixed * scale, axis=0) / jnp.sum(total * scale, axis=0)
    twice = jnp.concatenate([done, done], axis=0)
    twice = jnp.where(iota((16, 32), 0) // 8 == iota((16, 32), 1) // 16, twice, 0.0).astype(BF)
    fold = (iota((32, 16), 0) % 16 == iota((32, 16), 1)).astype(BF)
    final = dot(twice, fold, ((1,), (0,))).astype(BF)
    context[...] = final
    term = dot(final, out_proj[...], ((1,), (0,))).astype(BF)
    for k in range(PLANE):
        out[k] = term[:, k * 128 : (k + 1) * 128]


def sum_plane(arrived, out):
    total = jnp.sum(arrived[...].astype(F32), axis=0).astype(BF)
    for z in range(Z):
        out[z] = total


def make_mid(arrived, hidden_block, out):
    mid = (jnp.sum(arrived[...].astype(F32), axis=0) + hidden_block[...]).astype(BF)
    for k in range(PLANE):
        out[k] = mid


def experts(place, mid_blocks, gain, expert_ids, route_weights, w_gate, w_up, w_down, order, out):
    expert = place[4]
    ids = dot(expert_ids[...].astype(F32), eye(B, F32), ((0,), (0,)))
    exact = lax.Precision.HIGHEST
    routes = dot(route_weights[...], eye(B, F32), ((0,), (0,)), exact)
    match = ids == expert.astype(F32)
    hits = jnp.sum(match.astype(F32), axis=0, keepdims=True)
    share = routes / jnp.sum(routes, axis=0, keepdims=True)
    weight = jnp.sum(jnp.where(match, share, 0.0), axis=0, keepdims=True)
    before = (iota((B, B), 0) < iota((B, B), 1)).astype(F32)
    rank = dot(jnp.broadcast_to(hits, (8, B)), before, ((1,), (0,)))
    table = (hits > 0.5) & (jnp.abs(rank - iota((8, B), 0).astype(F32)) < 0.5)
    coefficient = jnp.sum(jnp.where(table, weight, 0.0), axis=1, keepdims=True)
    table = table.astype(BF)
    mid = jnp.concatenate([mid_blocks[k] for k in range(PLANE)], axis=1)
    rows = dot(table, mid, ((1,), (0,)))
    scale = lax.rsqrt(jnp.sum(rows * rows, axis=1, keepdims=True) * (1.0 / D) + 1e-06)
    picked = (rows * scale * gain[...].astype(F32)).astype(BF)
    gate = dot(picked, w_gate[...], ((1,), (1,)))
    upward = dot(picked, w_up[...], ((1,), (1,)))
    hidden_units = (gate / (1.0 + jnp.exp(-gate)) * upward).astype(BF)
    weighted = (dot(hidden_units, w_down[...], ((1,), (0,))) * coefficient).astype(BF)
    back = dot(table, weighted, ((0,), (0,))).astype(BF)
    stacked = jnp.concatenate([back[:, x * 1024 : (x + 1) * 1024] for x in range(X)], axis=0)
    sorted_back = dot(stacked, order[...], ((1,), (0,))).astype(BF)
    for x in range(X):
        for c in range(CY):
            out[x * CY + c] = sorted_back[x * B : (x + 1) * B, c * 128 : (c + 1) * 128]


def sum_experts(arrived, out):
    total = jnp.sum(arrived[...].astype(F32), axis=0).astype(BF)
    turned = dot(eye(128), total, ((1,), (1,)))
    out[...] = turned.reshape(Z, 8, B).astype(BF)


def finish_layer(place, arrived, mid_blocks, out):
    x, z, cy = place[1], place[2], place[3]
    total = jnp.sum(arrived[...].astype(F32), axis=0)
    mixture = dot(total, eye(8, F32), ((0,), (0,)), lax.Precision.HIGHEST)
    tile = mid_blocks[x * CY + z // 2]
    select = iota((128, 8), 0) == z % 2 * 64 + cy * 8 + iota((128, 8), 1)
    mid = dot(tile, select.astype(BF), ((1,), (0,)))
    out[...] = (mid + mixture).astype(BF)


def call(body, outs, scalars, *arrays):
    smem = pl.BlockSpec(memory_space=pltpu.SMEM)
    vmem = pl.BlockSpec(memory_space=pltpu.VMEM)
    single = not isinstance(outs, list)
    results = pl.pallas_call(
        body,
        out_shape=outs,
        in_specs=[smem] * len(scalars) + [vmem] * len(arrays),
        out_specs=vmem if single else [vmem] * len(outs),
        compiler_params=pltpu.CompilerParams(vmem_limit_bytes=24 * 1024 * 1024),
    )(*scalars, *arrays)
    return results


def swap(blocks, axes):
    return lax.all_to_all(blocks, axes, 0, 0, tiled=True)


def block_order():
    columns = np.arange(1024).reshape(Z, CY, 8).transpose(1, 0, 2).reshape(-1)
    order = np.zeros((1024, 1024), np.float32)
    order[columns, np.arange(1024)] = 1.0
    return order.astype(jnp.bfloat16)


def shards(
    query,
    key_cache,
    value_cache,
    lengths,
    hidden_in,
    out_proj,
    norm_gain,
    expert_ids,
    route_weights,
    w_gate,
    w_up,
    w_down,
):
    x, z = lax.axis_index("x"), lax.axis_index("z")
    cy = lax.axis_index("c") * 4 + lax.axis_index("y")
    expert = x * Z + z
    place = jnp.stack([expert * CY + cy, x, z, cy, expert]).astype(jnp.int32)

    def shape(*dims, dtype=BF):
        return jax.ShapeDtypeStruct(dims, dtype)

    own = jnp.concatenate([query[:8], query[8:], hidden_in.T], axis=1)
    along_z = swap(jnp.broadcast_to(own[None], (Z, 8, 48)), "z")
    gathered = swap(call(spread_query, shape(PLANE, 48, 128), (), along_z), PLANE_AXES)
    partial, hidden_block = call(
        attend,
        [shape(PLANE, 48, 128), shape(B, 128, dtype=F32)],
        (place, lengths),
        gathered,
        key_cache,
        value_cache,
    )
    merged = call(merge_plane, shape(Z, 8, 48), (), swap(partial, PLANE_AXES))
    context, term = call(
        finish_context,
        [shape(B, 16), shape(PLANE, B, 128)],
        (),
        swap(merged, "z"),
        out_proj,
    )
    projected = call(sum_plane, shape(Z, B, 128), (), swap(term, PLANE_AXES))
    mid = call(make_mid, shape(PLANE, B, 128), (), swap(projected, "z"), hidden_block)
    mid_blocks = swap(mid, PLANE_AXES)
    mixture = call(
        experts,
        shape(PLANE, B, 128),
        (place,),
        mid_blocks,
        norm_gain.reshape(1, D),
        expert_ids,
        route_weights,
        w_gate,
        w_up,
        w_down,
        jnp.asarray(block_order()),
    )
    summed = call(sum_experts, shape(Z, 8, B), (), swap(mixture, PLANE_AXES))
    layer_out = call(finish_layer, shape(B, 8), (place,), swap(summed, "z"), mid_blocks)
    return context, layer_out


def solution(mesh):
    fine = Mesh(np.asarray(mesh.devices).reshape(X, Z, 2, 4), ALL_AXES)
    columns, rows = P(None, ALL_AXES), P(ALL_AXES, None)
    cache = P(None, ALL_AXES, None)
    placed = (
        columns,
        cache,
        cache,
        P(),
        columns,
        rows,
        P(),
        P(),
        P(),
        rows,
        rows,
        rows,
    )
    return jax.shard_map(
        shards,
        mesh=fine,
        in_specs=placed,
        out_specs=(columns, columns),
        check_vma=False,
    )
```

```python
import math

import jax
import jax.numpy as jnp
import numpy as np
from jax import lax
from jax.experimental import pallas as pl
from jax.experimental.pallas import tpu as pltpu
from jax.sharding import Mesh
from jax.sharding import PartitionSpec as P

HD = 128
X, Z, CY = 4, 16, 8
PLANE = X * CY
B = 16
D = 4096
COLS = D // Z
SPAN = 32
FLOOR = -1e30
BF = jnp.bfloat16
F32 = jnp.float32
PLANE_AXES = ("x", "c", "y")
ALL_AXES = ("x", "z", "c", "y")
EXACT = lax.Precision.HIGHEST


def iota(shape, dimension):
    return lax.broadcasted_iota(jnp.int32, shape, dimension)


def dot(a, b, dims, precision=None):
    return lax.dot_general(
        a, b, (dims, ((), ())), preferred_element_type=F32, precision=precision
    )


def eye(n, dtype=BF):
    return (iota((n, n), 0) == iota((n, n), 1)).astype(dtype)


def halves(first, second, high):
    low_lanes = iota(first.shape, 1) < 64
    if high:
        return jnp.where(low_lanes, pltpu.roll(first, 64, 1), second)
    return jnp.where(low_lanes, first, pltpu.roll(second, 64, 1))


def deal_out(query, out_proj, out, held, sem):
    copy = pltpu.make_async_copy(out_proj, held, sem)
    copy.start()
    place = (iota((16, 128), 0) == iota((16, 128), 1)).astype(BF)
    wide = dot(query[...], place, ((1,), (0,))).astype(BF)
    copy.wait()
    for v in range(Z // 2):
        tiles = [
            held[:, x * 1024 + v * 128 : x * 1024 + (v + 1) * 128].astype(F32) for x in range(X)
        ]
        for high in range(2):
            z = 2 * v + high
            out[z, :, 0:128] = halves(tiles[0], tiles[1], high).astype(BF)
            out[z, :, 128:256] = halves(tiles[2], tiles[3], high).astype(BF)
            out[z, :, 256:384] = wide


def spread_query(arrived, out):
    rows = arrived[:, :, 256:384].astype(F32)
    unit = eye(128)
    parts = []
    for i in range(2):
        part = rows[:, i * 8 : (i + 1) * 8, :].reshape(128, 128).astype(BF)
        parts.append(dot(part, unit, ((0,), (0,)))[:16])
    turned = jnp.concatenate(parts, axis=0).astype(BF)
    for k in range(PLANE):
        out[k] = turned


def attend(place, lengths, gathered, hidden, keys, values, out, held_keys, held_values, sems):
    copies = []
    for i in range(2):
        part = pl.ds(i * 8, 8)
        copies.append(
            [
                pltpu.make_async_copy(keys.at[part], held_keys.at[part], sems.at[i, 0]),
                pltpu.make_async_copy(values.at[part], held_values.at[part], sems.at[i, 1]),
            ]
        )
        for copy in copies[i]:
            copy.start()
    device = place[0]
    lane_j = iota((SPAN, 128), 1) % 8
    position = device * SPAN + iota((SPAN, 128), 0)
    spot = (iota((B, 128), 0) == iota((B, 128), 1) % B).astype(BF)
    repeated = dot(hidden[...], spot, ((1,), (0,)))
    own = jnp.where(iota((8, 128), 0) == iota((8, 128), 1) // B, repeated, 0.0)
    own = jnp.sum(own, axis=0, keepdims=True)
    zeros = jnp.zeros((9, 128), F32)
    stats = [[None] * 6 for _ in range(X)]
    for i in range(2):
        valid = jnp.concatenate(
            [
                ((lane_j == j) & (position < lengths[i * 8 + j])).astype(F32)
                for j in range(8)
            ],
            axis=0,
        )
        valid = valid > 0.5
        copies[i][0].wait()
        copies[i][1].wait()
        for g in range(X):
            query = gathered[g * CY : (g + 1) * CY, i * 16 : (i + 1) * 16, :].reshape(HD, 128)
            k = held_keys[i * 8 : (i + 1) * 8, :, g * HD : (g + 1) * HD].reshape(8 * SPAN, HD)
            v = held_values[i * 8 : (i + 1) * 8, :, g * HD : (g + 1) * HD].reshape(8 * SPAN, HD)
            scores = dot(k, query, ((1,), (0,))) * (1.0 / math.sqrt(HD))
            scores = jnp.where(valid, scores, FLOOR)
            top = jnp.max(scores, axis=0, keepdims=True).astype(BF).astype(F32)
            weights = jnp.where(valid, jnp.exp(scores - top), 0.0).astype(BF)
            total = jnp.sum(weights.astype(F32), axis=0, keepdims=True)
            mixed = dot(v, weights, ((0,), (0,))).astype(BF)
            for c in range(CY):
                out[g * CY + c, i * 16 : (i + 1) * 16, :] = mixed[c * 16 : (c + 1) * 16]
            high = total.astype(BF).astype(F32)
            stats[g][i] = top
            stats[g][2 + i] = high
            stats[g][4 + i] = total - high
    for g in range(X):
        block = jnp.concatenate(stats[g] + [own, zeros], axis=0).astype(BF)
        for c in range(CY):
            out[g * CY + c, 32:48, :] = block


def merge(arrived, i):
    top = arrived[:, 32 + i, :].astype(F32)
    total = arrived[:, 34 + i, :].astype(F32) + arrived[:, 36 + i, :].astype(F32)
    best = jnp.max(top, axis=0, keepdims=True)
    scale = jnp.exp(top - best)
    mass = jnp.sum(total * scale, axis=0, keepdims=True)
    mixed = arrived[:, i * 16 : (i + 1) * 16, :].astype(F32)
    return jnp.sum(mixed * scale[:, None, :], axis=0), best, mass


def merge_plane(arrived, out, hidden_cols):
    parts, tops, highs, lows = [], [], [], []
    for i in range(2):
        mixed, best, mass = merge(arrived, i)
        high = mass.astype(BF).astype(F32)
        parts.append(mixed)
        tops.append(best)
        highs.append(high)
        lows.append(mass - high)
    full = jnp.concatenate(
        parts + tops + highs + lows + [jnp.zeros((10, 128), F32)], axis=0
    ).astype(BF)
    for z in range(Z):
        out[z] = full
    owned = arrived[:, 38, :].astype(F32).astype(BF)
    for t in range(2):
        put = (iota((16, 128), 0) == iota((16, 128), 1) // 8).astype(BF)
        by_lane = dot(owned[t * 16 : (t + 1) * 16], put, ((0,), (0,)))
        mine = iota((128, 128), 0) // B == iota((128, 128), 1) % 8
        by_lane = jnp.where(mine, by_lane, 0.0).reshape(8, B, 128)
        hidden_cols[:, t * 128 : (t + 1) * 128] = jnp.sum(by_lane, axis=0)


def finish_context(place, arrived, dealt, context, out):
    z = place[2]
    weights = dealt[:, :, 0:COLS].reshape(Z * 16, COLS)
    contexts, terms = [], []
    for i in range(2):
        mixed, _, mass = merge(arrived, i)
        done = (mixed / mass).astype(BF)
        mine = (iota((8, 128), 1) == z * 8 + iota((8, 128), 0)).astype(BF)
        contexts.append(dot(mine, done, ((1,), (1,))))
        tile = (iota((16, 256), 0) == iota((16, 256), 1) % 16).astype(BF)
        tiled = dot(done, tile, ((0,), (0,)))
        block = iota((128, 256), 0) // 8 == iota((128, 256), 1) // 16
        tiled = jnp.where(block, tiled, 0.0).astype(BF)
        term = dot(tiled, weights, ((1,), (0,)))
        terms.append(jnp.sum(term.reshape(Z, 8, COLS), axis=0))
    context[...] = jnp.concatenate(contexts, axis=0).astype(BF)
    term = jnp.concatenate(terms, axis=0).astype(BF)
    for k in range(PLANE):
        out[k] = term


def slots(ids, expert, rows):
    hits = jnp.zeros((rows, B), F32)
    for k in range(8):
        hits += (ids[k : k + 1, :] == expert).astype(F32)
    before = (iota((B, B), 0) < iota((B, B), 1)).astype(BF)
    rank = dot(hits.astype(BF), before, ((1,), (0,)))
    return (hits > 0.5) & (jnp.abs(rank - (iota((rows, B), 0) % 8).astype(F32)) < 0.5)


def make_mid(place, arrived, hidden_cols, expert_ids, out, mid_part):
    x, cy = place[1], place[3]
    projected = jnp.sum(arrived[...].astype(F32), axis=0)
    mid = (projected + hidden_cols[...]).astype(BF)
    expert = x * Z + iota((128, B), 0) // 8
    table = slots(expert_ids[...], expert, 128).astype(BF)
    picked = dot(table, mid, ((1,), (0,)))
    parts = [picked[:, t * 128 : (t + 1) * 128].reshape(Z, 8, 128) for t in range(2)]
    out[...] = jnp.concatenate(parts, axis=1).astype(BF)
    mine = iota((8, COLS), 1) == x * 64 + cy * 8 + iota((8, COLS), 0)
    mid_part[...] = dot(mine.astype(BF), mid, ((1,), (1,)))


def experts(
    place, arrived, gain, expert_ids, route_weights, w_gate, order, w_up, w_down, out,
    held_up, held_down, sems,
):
    up_copy = pltpu.make_async_copy(w_up, held_up, sems.at[0])
    down_copy = pltpu.make_async_copy(w_down, held_down, sems.at[1])
    up_copy.start()
    down_copy.start()
    expert = place[4]
    ids = expert_ids[...]
    routes = route_weights[...]
    table = slots(ids, expert, 8)
    share = routes / jnp.sum(routes, axis=0, keepdims=True)
    weight = jnp.sum(jnp.where(ids == expert, share, 0.0), axis=0, keepdims=True)
    coefficient = jnp.sum(jnp.where(table, weight, 0.0), axis=1, keepdims=True)
    table = table.astype(BF)
    tiles = []
    for x in range(X):
        t = x // 2
        for v in range(Z // 2):
            first = arrived[2 * v].astype(F32)[t * 8 : (t + 1) * 8]
            second = arrived[2 * v + 1].astype(F32)[t * 8 : (t + 1) * 8]
            tiles.append(halves(first, second, x % 2))
    rows = jnp.concatenate(tiles, axis=1)
    scale = lax.rsqrt(jnp.sum(rows * rows, axis=1, keepdims=True) * (1.0 / D) + 1e-06)
    picked = (rows * scale * gain[...].astype(F32)).astype(BF)
    gate = dot(picked, w_gate[...], ((1,), (1,)))
    up_copy.wait()
    upward = dot(picked, held_up[...], ((1,), (1,)))
    hidden_units = (gate / (1.0 + jnp.exp(-gate)) * upward).astype(BF)
    down_copy.wait()
    weighted = (dot(hidden_units, held_down[...], ((1,), (0,))) * coefficient).astype(BF)
    back = dot(table, weighted, ((0,), (0,))).astype(BF)
    stacked = jnp.concatenate([back[:, x * 1024 : (x + 1) * 1024] for x in range(X)], axis=0)
    sorted_back = dot(stacked, order[...], ((1,), (0,))).astype(BF)
    for x in range(X):
        for c in range(CY):
            out[x * CY + c] = sorted_back[x * B : (x + 1) * B, c * 128 : (c + 1) * 128]


def sum_experts(arrived, out):
    total = jnp.sum(arrived[...].astype(F32), axis=0).astype(BF)
    turned = dot(eye(128), total, ((1,), (1,)))
    out[...] = turned.reshape(Z, 8, B).astype(BF)


def finish_layer(arrived, mid_part, out):
    out[...] = (mid_part[...] + jnp.sum(arrived[...].astype(F32), axis=0)).astype(BF)


def call(body, outs, scalars, arrays, far=(), scratch=()):
    smem = pl.BlockSpec(memory_space=pltpu.SMEM)
    vmem = pl.BlockSpec(memory_space=pltpu.VMEM)
    anywhere = pl.BlockSpec(memory_space=pl.ANY)
    single = not isinstance(outs, list)
    return pl.pallas_call(
        body,
        out_shape=outs,
        in_specs=[smem] * len(scalars) + [vmem] * len(arrays) + [anywhere] * len(far),
        out_specs=vmem if single else [vmem] * len(outs),
        scratch_shapes=list(scratch),
        compiler_params=pltpu.CompilerParams(vmem_limit_bytes=24 * 1024 * 1024),
    )(*scalars, *arrays, *far)


def swap(blocks, axes):
    return lax.all_to_all(blocks, axes, 0, 0, tiled=True)


def block_order():
    columns = np.arange(1024).reshape(Z, CY, 8).transpose(1, 0, 2).reshape(-1)
    order = np.zeros((1024, 1024), np.float32)
    order[columns, np.arange(1024)] = 1.0
    return order.astype(jnp.bfloat16)


def shards(
    query,
    key_cache,
    value_cache,
    lengths,
    hidden_in,
    out_proj,
    norm_gain,
    expert_ids,
    route_weights,
    w_gate,
    w_up,
    w_down,
):
    x, z = lax.axis_index("x"), lax.axis_index("z")
    cy = lax.axis_index("c") * 4 + lax.axis_index("y")
    expert = x * Z + z
    place = jnp.stack([expert * CY + cy, x, z, cy, expert]).astype(jnp.int32)
    ids, routes = expert_ids.T, route_weights.T
    dma = pltpu.SemaphoreType.DMA

    def shape(*dims, dtype=BF):
        return jax.ShapeDtypeStruct(dims, dtype)

    dealt = swap(
        call(
            deal_out,
            shape(Z, 16, COLS + 128),
            (),
            (query,),
            (out_proj,),
            (pltpu.VMEM((16, D), BF), dma),
        ),
        "z",
    )
    gathered = swap(call(spread_query, shape(PLANE, 32, 128), (), (dealt,)), PLANE_AXES)
    partial = call(
        attend,
        shape(PLANE, 48, 128),
        (place, lengths),
        (gathered, hidden_in.T),
        (key_cache, value_cache),
        (pltpu.VMEM((B, SPAN, 512), BF), pltpu.VMEM((B, SPAN, 512), BF), dma((2, 2))),
    )
    merged, hidden_cols = call(
        merge_plane,
        [shape(Z, 48, 128), shape(B, COLS, dtype=F32)],
        (),
        (swap(partial, PLANE_AXES),),
    )
    context, term = call(
        finish_context,
        [shape(B, 16), shape(PLANE, B, COLS)],
        (place,),
        (swap(merged, "z"), dealt),
    )
    picked, mid_part = call(
        make_mid,
        [shape(Z, 16, 128), shape(8, B, dtype=F32)],
        (place,),
        (swap(term, PLANE_AXES), hidden_cols, ids),
    )
    mixture = call(
        experts,
        shape(PLANE, B, 128),
        (place,),
        (
            swap(picked, "z"),
            norm_gain.reshape(1, D),
            ids,
            routes,
            w_gate,
            jnp.asarray(block_order()),
        ),
        (w_up, w_down),
        (pltpu.VMEM((128, D), BF), pltpu.VMEM((128, D), BF), dma((2,))),
    )
    summed = call(sum_experts, shape(Z, 8, B), (), (swap(mixture, PLANE_AXES),))
    layer_out = call(finish_layer, shape(8, B), (), (swap(summed, "z"), mid_part))
    return context, layer_out.T


def solution(mesh):
    fine = Mesh(np.asarray(mesh.devices).reshape(X, Z, 2, 4), ALL_AXES)
    columns, rows = P(None, ALL_AXES), P(ALL_AXES, None)
    cache = P(None, ALL_AXES, None)
    placed = (
        columns,
        cache,
        cache,
        P(),
        columns,
        rows,
        P(),
        P(),
        P(),
        rows,
        rows,
        rows,
    )
    return jax.shard_map(
        shards,
        mesh=fine,
        in_specs=placed,
        out_specs=(columns, columns),
        check_vma=False,
    )
```

```python
import math

import jax
import jax.numpy as jnp
import numpy as np
from jax import lax
from jax.experimental import pallas as pl
from jax.experimental.pallas import tpu as pltpu
from jax.sharding import Mesh
from jax.sharding import PartitionSpec as P

HD = 128
X, Z, CY = 4, 16, 8
PLANE = X * CY
B = 16
D = 4096
COLS = D // Z
SPAN = 32
FLOOR = -1e30
BF = jnp.bfloat16
F32 = jnp.float32
PLANE_AXES = ("x", "c", "y")
ALL_AXES = ("x", "z", "c", "y")
EXACT = lax.Precision.HIGHEST


def iota(shape, dimension):
    return lax.broadcasted_iota(jnp.int32, shape, dimension)


def dot(a, b, dims, precision=None):
    return lax.dot_general(
        a, b, (dims, ((), ())), preferred_element_type=F32, precision=precision
    )


def eye(n, dtype=BF):
    return (iota((n, n), 0) == iota((n, n), 1)).astype(dtype)


def halves(first, second, high):
    low_lanes = iota(first.shape, 1) < 64
    if high:
        return jnp.where(low_lanes, pltpu.roll(first, 64, 1), second)
    return jnp.where(low_lanes, first, pltpu.roll(second, 64, 1))


def coordinates():
    x, z = lax.axis_index("x"), lax.axis_index("z")
    return x, z, lax.axis_index("c") * 4 + lax.axis_index("y")


def deal_out(query, out_proj, out, held_query, held, sems):
    copies = [
        pltpu.make_async_copy(query, held_query, sems.at[0]),
        pltpu.make_async_copy(out_proj, held, sems.at[1]),
    ]
    for copy in copies:
        copy.start()
    copies[0].wait()
    own = held_query[...]
    parts = []
    for i in range(2):
        put = (iota((16, 128), 0) + i * 16 == iota((16, 128), 1)).astype(BF)
        parts.append(dot(own, put, ((1,), (0,)))[i * 8 : (i + 1) * 8])
    wide = parts[0] + parts[1]
    copies[1].wait()
    for v in range(Z // 2):
        tiles = [
            held[:, x * 1024 + v * 128 : x * 1024 + (v + 1) * 128].astype(F32) for x in range(X)
        ]
        for high in range(2):
            pieces = [halves(tiles[0], tiles[1], high), halves(tiles[2], tiles[3], high), wide]
            out[2 * v + high] = jnp.concatenate(pieces, axis=0).astype(BF)


def spread_query(arrived, out):
    rows = arrived[:, 32:40, :].astype(F32).reshape(128, 128).astype(BF)
    turned = dot(rows, eye(128), ((0,), (0,)))[:32].astype(BF)
    for k in range(PLANE):
        out[k] = turned


def attend(gathered, keys, values, hidden, lengths, out, held_lengths, sem):
    copy = pltpu.make_async_copy(lengths, held_lengths, sem)
    copy.start()
    x, z, cy = coordinates()
    device = (x * Z + z) * CY + cy
    lane_j = iota((SPAN, 128), 1) % 8
    position = device * SPAN + iota((SPAN, 128), 0)
    spot = (iota((B, 128), 0) == iota((B, 128), 1) % B).astype(BF)
    repeated = dot(hidden[...], spot, ((1,), (0,)))
    own = jnp.where(iota((8, 128), 0) == iota((8, 128), 1) // B, repeated, 0.0)
    own = jnp.sum(own, axis=0, keepdims=True)
    zero = jnp.zeros((1, 128), F32)
    copy.wait()
    valids = []
    for i in range(2):
        rows = [(lane_j == j) & (position < held_lengths[i * 8 + j]) for j in range(8)]
        valids.append(jnp.concatenate([r.astype(F32) for r in rows], axis=0) > 0.5)
    for g in range(X):
        parts, tops, highs, lows = [], [], [], []
        for i in range(2):
            query = gathered[g * CY : (g + 1) * CY, i * 16 : (i + 1) * 16, :].reshape(HD, 128)
            k = keys[i * 8 : (i + 1) * 8, :, g * HD : (g + 1) * HD].reshape(8 * SPAN, HD)
            v = values[i * 8 : (i + 1) * 8, :, g * HD : (g + 1) * HD].reshape(8 * SPAN, HD)
            scores = dot(k, query, ((1,), (0,))) * (1.0 / math.sqrt(HD))
            scores = jnp.where(valids[i], scores, FLOOR)
            top = jnp.max(scores, axis=0, keepdims=True).astype(BF).astype(F32)
            weights = jnp.where(valids[i], jnp.exp(scores - top), 0.0).astype(BF)
            total = jnp.sum(weights.astype(F32), axis=0, keepdims=True)
            high = total.astype(BF).astype(F32)
            parts.append(dot(v, weights, ((0,), (0,))))
            tops.append(top)
            highs.append(high)
            lows.append(total - high)
        block = jnp.concatenate(tops + highs + lows + [own, zero], axis=0)
        for c in range(CY):
            pieces = [part[c * 16 : (c + 1) * 16] for part in parts]
            out[g * CY + c] = jnp.concatenate(pieces + [block], axis=0).astype(BF)


def merge(arrived, i):
    top = arrived[:, 32 + i, :].astype(F32)
    total = arrived[:, 34 + i, :].astype(F32) + arrived[:, 36 + i, :].astype(F32)
    best = jnp.max(top, axis=0, keepdims=True)
    scale = jnp.exp(top - best)
    mass = jnp.sum(total * scale, axis=0, keepdims=True)
    mixed = arrived[:, i * 16 : (i + 1) * 16, :].astype(F32)
    return jnp.sum(mixed * scale[:, None, :], axis=0), best, mass


def merge_plane(arrived, out, hidden_cols):
    parts, tops, highs, lows = [], [], [], []
    for i in range(2):
        mixed, best, mass = merge(arrived, i)
        high = mass.astype(BF).astype(F32)
        parts.append(mixed)
        tops.append(best)
        highs.append(high)
        lows.append(mass - high)
    full = jnp.concatenate(
        parts + tops + highs + lows + [jnp.zeros((2, 128), F32)], axis=0
    ).astype(BF)
    for z in range(Z):
        out[z] = full
    owned = arrived[:, 38, :].astype(F32).astype(BF)
    for t in range(2):
        put = (iota((16, 128), 0) == iota((16, 128), 1) // 8).astype(BF)
        by_lane = dot(owned[t * 16 : (t + 1) * 16], put, ((0,), (0,)))
        mine = iota((128, 128), 0) // B == iota((128, 128), 1) % 8
        by_lane = jnp.where(mine, by_lane, 0.0).reshape(8, B, 128)
        hidden_cols[:, t * 128 : (t + 1) * 128] = jnp.sum(by_lane, axis=0)


def finish_context(arrived, dealt, context, out):
    z = lax.axis_index("z")
    weights = jnp.concatenate(
        [dealt[:, t * 16 : (t + 1) * 16, :].reshape(Z * 16, 128) for t in range(2)], axis=1
    )
    contexts, terms = [], []
    for i in range(2):
        mixed, _, mass = merge(arrived, i)
        done = (mixed / mass).astype(BF)
        mine = (iota((8, 128), 1) == z * 8 + iota((8, 128), 0)).astype(BF)
        contexts.append(dot(mine, done, ((1,), (1,))))
        tile = (iota((16, 256), 0) == iota((16, 256), 1) % 16).astype(BF)
        tiled = dot(done, tile, ((0,), (0,)))
        block = iota((128, 256), 0) // 8 == iota((128, 256), 1) // 16
        tiled = jnp.where(block, tiled, 0.0).astype(BF)
        term = dot(tiled, weights, ((1,), (0,)))
        terms.append(jnp.sum(term.reshape(Z, 8, COLS), axis=0))
    context[...] = jnp.concatenate(contexts, axis=0).astype(BF)
    term = jnp.concatenate(terms, axis=0).astype(BF)
    for k in range(PLANE):
        out[k] = term


def slots(ids, expert, slot):
    hits = jnp.zeros(slot.shape, F32)
    for k in range(8):
        hits += (ids[k : k + 1, :] == expert).astype(F32)
    before = (iota((B, B), 0) < iota((B, B), 1)).astype(BF)
    rank = dot(hits.astype(BF), before, ((1,), (0,)))
    return (hits > 0.5) & (jnp.abs(rank - slot.astype(F32)) < 0.5)


def make_mid(arrived, hidden_cols, expert_ids, out, mid_part):
    x, _, cy = coordinates()
    projected = jnp.sum(arrived[...].astype(F32), axis=0)
    mid = (projected + hidden_cols[...]).astype(BF)
    row = iota((128, B), 0)
    table = slots(expert_ids[...], x * Z + row // 8, row % 4)
    picked = jnp.zeros((128, 128), F32)
    for t in range(2):
        half = (table & (row // 4 % 2 == t)).astype(BF)
        picked += dot(half, mid[:, t * 128 : (t + 1) * 128], ((1,), (0,)))
    out[...] = picked.reshape(Z, 8, 128).astype(BF)
    mine = iota((8, COLS), 1) == x * 64 + cy * 8 + iota((8, COLS), 0)
    mid_part[...] = dot(mine.astype(BF), mid, ((1,), (1,)))


def sort_columns(tiles):
    lane = iota((8, 128), 1)
    for bit in (32, 16, 8):
        low = lane // bit % 2 == 0
        high = lane // (2 * bit) % 2 == 0
        tiles = [
            jnp.where(
                low == high,
                tile,
                jnp.where(high, pltpu.roll(tile, 128 - bit, 1), pltpu.roll(tile, bit, 1)),
            )
            for tile in tiles
        ]
    for step in (4, 2, 1):
        low = lane // (16 * step) % 2 == 0
        swapped = list(tiles)
        for v in range(8):
            if v & step == 0:
                first, second = tiles[v], tiles[v + step]
                swapped[v] = jnp.where(low, first, pltpu.roll(second, 16 * step, 1))
                swapped[v + step] = jnp.where(low, pltpu.roll(first, 128 - 16 * step, 1), second)
        tiles = swapped
    return tiles


def experts(arrived, gain, expert_ids, route_weights, w_gate, w_up, w_down, out):
    x, z, _ = coordinates()
    expert = x * Z + z
    ids = expert_ids[...]
    routes = route_weights[...]
    table = slots(ids, expert, iota((8, B), 0))
    share = routes / jnp.sum(routes, axis=0, keepdims=True)
    weight = jnp.sum(jnp.where(ids == expert, share, 0.0), axis=0, keepdims=True)
    coefficient = jnp.sum(jnp.where(table, weight, 0.0), axis=1, keepdims=True)
    first_half = iota((8, 128), 0) < 4
    gains = gain[...].astype(F32)
    tiles, scaled = [], []
    for p in range(2):
        for v in range(Z // 2):
            tile = halves(arrived[2 * v].astype(F32), arrived[2 * v + 1].astype(F32), p)
            low, high = p * 8 + v, (2 + p) * 8 + v
            tiles.append(tile * tile)
            scaled.append(
                tile * jnp.where(first_half, gains[low : low + 1], gains[high : high + 1])
            )
    squares = sum(tiles[1:], tiles[0])
    squares = squares + jnp.concatenate([squares[4:], squares[:4]], axis=0)
    scale = lax.rsqrt(jnp.sum(squares, axis=1, keepdims=True) * (1.0 / D) + 1e-06)
    picked = jnp.concatenate([(tile * scale).astype(BF) for tile in scaled], axis=1)

    def project(weights):
        near = dot(picked, weights[:, : D // 2], ((1,), (1,)))
        far = dot(picked, weights[:, D // 2 :], ((1,), (1,)))
        return near + jnp.concatenate([far[4:], far[:4]], axis=0)

    gate = project(w_gate)
    upward = project(w_up)
    hidden_units = (gate / (1.0 + jnp.exp(-gate)) * upward).astype(BF)
    weighted = dot(hidden_units, w_down[...], ((1,), (0,))) * coefficient
    for group in range(X):
        start = group * 1024
        tiles = [weighted[:, start + v * 128 : start + (v + 1) * 128] for v in range(8)]
        for c, tile in enumerate(sort_columns(tiles)):
            out[group * CY + c] = tile.astype(BF)


def sum_experts(arrived, expert_ids, out):
    z = lax.axis_index("z")
    parts = [
        jnp.sum(arrived[x * CY : (x + 1) * CY].astype(F32), axis=0) for x in range(X)
    ]
    row = iota((8 * X, B), 0)
    table = slots(expert_ids[...], row // 8 * Z + z, row % 8).astype(F32)
    turned = dot(jnp.concatenate(parts, axis=0), table, ((0,), (0,)), EXACT)
    out[...] = turned.reshape(Z, 8, B).astype(BF)


def finish_layer(arrived, mid_part, out):
    out[...] = (mid_part[...] + jnp.sum(arrived[...].astype(F32), axis=0)).astype(BF)


def call(body, outs, arrays, far=(), scratch=(), limit=16):
    vmem = pl.BlockSpec(memory_space=pltpu.VMEM)
    remote = pl.BlockSpec(memory_space=pltpu.HBM)
    single = not isinstance(outs, list)
    return pl.pallas_call(
        body,
        out_shape=outs,
        in_specs=[vmem] * len(arrays) + [remote] * len(far),
        out_specs=vmem if single else [vmem] * len(outs),
        scratch_shapes=list(scratch),
        compiler_params=pltpu.CompilerParams(vmem_limit_bytes=limit * 1024 * 1024),
    )(*arrays, *far)


def swap(blocks, axes):
    return lax.all_to_all(blocks, axes, 0, 0, tiled=True)


def shards(
    query,
    key_cache,
    value_cache,
    lengths,
    hidden_in,
    out_proj,
    norm_gain,
    expert_ids,
    route_weights,
    w_gate,
    w_up,
    w_down,
):
    ids, routes = expert_ids.T, route_weights.T
    dma, vmem = pltpu.SemaphoreType.DMA, pltpu.VMEM

    def shape(*dims, dtype=BF):
        return jax.ShapeDtypeStruct(dims, dtype)

    dealt = swap(
        call(
            deal_out,
            shape(Z, 40, 128),
            (),
            (query, out_proj),
            (vmem((B, 16), BF), vmem((16, D), BF), dma((2,))),
            62,
        ),
        "z",
    )
    gathered = swap(call(spread_query, shape(PLANE, 32, 128), (dealt,)), PLANE_AXES)
    partial = call(
        attend,
        shape(PLANE, 40, 128),
        (gathered, key_cache, value_cache, hidden_in.T),
        (lengths,),
        (pltpu.SMEM((B,), jnp.int32), dma),
    )
    merged, hidden_cols = call(
        merge_plane,
        [shape(Z, 40, 128), shape(B, COLS, dtype=F32)],
        (swap(partial, PLANE_AXES),),
    )
    context, term = call(
        finish_context,
        [shape(B, 16), shape(PLANE, B, COLS)],
        (swap(merged, "z"), dealt),
    )
    picked, mid_part = call(
        make_mid,
        [shape(Z, 8, 128), shape(8, B, dtype=F32)],
        (swap(term, PLANE_AXES), hidden_cols, ids),
    )
    mixture = call(
        experts,
        shape(PLANE, 8, 128),
        (swap(picked, "z"), norm_gain.reshape(PLANE, 128), ids, routes, w_gate, w_up, w_down),
    )
    summed = call(sum_experts, shape(Z, 8, B), (swap(mixture, PLANE_AXES), ids))
    layer_out = call(finish_layer, shape(8, B), (swap(summed, "z"), mid_part))
    return context, layer_out.T


def solution(mesh):
    fine = Mesh(np.asarray(mesh.devices).reshape(X, Z, 2, 4), ALL_AXES)
    columns, rows = P(None, ALL_AXES), P(ALL_AXES, None)
    cache = P(None, ALL_AXES, None)
    placed = (
        columns,
        cache,
        cache,
        P(),
        columns,
        rows,
        P(),
        P(),
        P(),
        rows,
        rows,
        rows,
    )
    return jax.shard_map(
        shards,
        mesh=fine,
        in_specs=placed,
        out_specs=(columns, columns),
        check_vma=False,
    )
```

```python
import math

import jax
import jax.numpy as jnp
import numpy as np
from jax import lax
from jax.experimental import pallas as pl
from jax.experimental.pallas import tpu as pltpu
from jax.sharding import Mesh
from jax.sharding import PartitionSpec as P

HD = 128
X, Z, CY = 4, 16, 8
PLANE = X * CY
B = 16
D = 4096
COLS = D // Z
SPAN = 32
FLOOR = -1e30
BF = jnp.bfloat16
F32 = jnp.float32
PLANE_AXES = ("x", "c", "y")
ALL_AXES = ("x", "z", "c", "y")
EXACT = lax.Precision.HIGHEST


def iota(shape, dimension):
    return lax.broadcasted_iota(jnp.int32, shape, dimension)


def dot(a, b, dims, precision=None):
    return lax.dot_general(
        a, b, (dims, ((), ())), preferred_element_type=F32, precision=precision
    )


def eye(n, dtype=BF):
    return (iota((n, n), 0) == iota((n, n), 1)).astype(dtype)


def halves(first, second, high):
    low_lanes = iota(first.shape, 1) < 64
    if high:
        return jnp.where(low_lanes, pltpu.roll(first, 64, 1), second)
    return jnp.where(low_lanes, first, pltpu.roll(second, 64, 1))


def coordinates():
    x, z = lax.axis_index("x"), lax.axis_index("z")
    return x, z, lax.axis_index("c") * 4 + lax.axis_index("y")


def pack_query(query, lengths, out, limits, held_query, held_lengths, sems):
    copies = [
        pltpu.make_async_copy(query, held_query, sems.at[0]),
        pltpu.make_async_copy(lengths, held_lengths, sems.at[1]),
    ]
    for copy in copies:
        copy.start()
    copies[0].wait()
    own = held_query[...]
    parts = []
    for i in range(2):
        put = (iota((16, 128), 0) + i * 16 == iota((16, 128), 1)).astype(BF)
        parts.append(dot(own, put, ((1,), (0,)))[i * 8 : (i + 1) * 8])
    wide = (parts[0] + parts[1]).astype(BF)
    for z in range(Z):
        out[z] = wide
    copies[1].wait()
    rows = [jnp.full((1, 128), held_lengths[b], jnp.int32) for b in range(B)]
    limits[...] = jnp.concatenate(rows, axis=0)


def spread_query(arrived, out):
    rows = arrived[...].astype(F32).reshape(128, 128).astype(BF)
    turned = dot(rows, eye(128), ((0,), (0,)))[:32].astype(BF)
    for k in range(PLANE):
        out[k] = turned


def attend(
    gathered, keys, values, hidden, limits, out, held_keys, held_values, held_hidden, held_limits, sems
):
    copies = [
        pltpu.make_async_copy(limits, held_limits, sems.at[0]),
        pltpu.make_async_copy(hidden, held_hidden, sems.at[1]),
    ]
    for n, (source, target) in enumerate(((keys, held_keys), (values, held_values))):
        for i in range(2):
            part = pl.ds(i * 8, 8)
            copies.append(
                pltpu.make_async_copy(source.at[part], target.at[part], sems.at[2 + 2 * n + i])
            )
    for copy in copies:
        copy.start()
    x, z, cy = coordinates()
    device = (x * Z + z) * CY + cy
    lane_j = iota((SPAN, 128), 1) % 8
    position = device * SPAN + iota((SPAN, 128), 0)
    copies[0].wait()
    copies[1].wait()
    spot = (iota((B, 128), 0) == iota((B, 128), 1) % B).astype(BF)
    repeated = dot(held_hidden[...], spot, ((1,), (0,)))
    own = jnp.where(iota((8, 128), 0) == iota((8, 128), 1) // B, repeated, 0.0)
    own = jnp.sum(own, axis=0, keepdims=True)
    zero = jnp.zeros((1, 128), F32)
    limit = held_limits[...]
    valids = []
    for i in range(2):
        rows = [
            (lane_j == j) & (position < limit[i * 8 + j : i * 8 + j + 1]) for j in range(8)
        ]
        valids.append(jnp.concatenate([r.astype(F32) for r in rows], axis=0) > 0.5)
    for copy in copies[2:]:
        copy.wait()
    for g in range(X):
        parts, tops, highs, lows = [], [], [], []
        for i in range(2):
            query = gathered[g * CY : (g + 1) * CY, i * 16 : (i + 1) * 16, :].reshape(HD, 128)
            k = held_keys[i * 8 : (i + 1) * 8, :, g * HD : (g + 1) * HD].reshape(8 * SPAN, HD)
            v = held_values[i * 8 : (i + 1) * 8, :, g * HD : (g + 1) * HD].reshape(8 * SPAN, HD)
            scores = dot(k, query, ((1,), (0,))) * (1.0 / math.sqrt(HD))
            scores = jnp.where(valids[i], scores, FLOOR)
            top = jnp.max(scores, axis=0, keepdims=True).astype(BF).astype(F32)
            weights = jnp.where(valids[i], jnp.exp(scores - top), 0.0).astype(BF)
            total = jnp.sum(weights.astype(F32), axis=0, keepdims=True)
            high = total.astype(BF).astype(F32)
            parts.append(dot(v, weights, ((0,), (0,))))
            tops.append(top)
            highs.append(high)
            lows.append(total - high)
        block = jnp.concatenate(tops + highs + lows + [own, zero], axis=0)
        for c in range(CY):
            pieces = [part[c * 16 : (c + 1) * 16] for part in parts]
            out[g * CY + c] = jnp.concatenate(pieces + [block], axis=0).astype(BF)


def merge(arrived, i):
    top = arrived[:, 32 + i, :].astype(F32)
    total = arrived[:, 34 + i, :].astype(F32) + arrived[:, 36 + i, :].astype(F32)
    best = jnp.max(top, axis=0, keepdims=True)
    scale = jnp.exp(top - best)
    mass = jnp.sum(total * scale, axis=0, keepdims=True)
    mixed = arrived[:, i * 16 : (i + 1) * 16, :].astype(F32)
    return jnp.sum(mixed * scale[:, None, :], axis=0), best, mass


def merge_plane(arrived, out, hidden_cols):
    parts, tops, highs, lows = [], [], [], []
    for i in range(2):
        mixed, best, mass = merge(arrived, i)
        high = mass.astype(BF).astype(F32)
        parts.append(mixed)
        tops.append(best)
        highs.append(high)
        lows.append(mass - high)
    full = jnp.concatenate(
        parts + tops + highs + lows + [jnp.zeros((2, 128), F32)], axis=0
    ).astype(BF)
    for z in range(Z):
        out[z] = full
    owned = arrived[:, 38, :].astype(F32).astype(BF)
    for t in range(2):
        put = (iota((16, 128), 0) == iota((16, 128), 1) // 8).astype(BF)
        by_lane = dot(owned[t * 16 : (t + 1) * 16], put, ((0,), (0,)))
        mine = iota((128, 128), 0) // B == iota((128, 128), 1) % 8
        by_lane = jnp.where(mine, by_lane, 0.0).reshape(8, B, 128)
        hidden_cols[:, t * 128 : (t + 1) * 128] = jnp.sum(by_lane, axis=0)


def finish_context(arrived, out_proj, context, out, weights, sems):
    z = lax.axis_index("z")
    copies = []
    for x in range(X):
        start = pl.multiple_of(x * 1024 + z // 2 * 128, 128)
        copies.append(
            pltpu.make_async_copy(
                out_proj.at[:, pl.ds(start, 128)],
                weights.at[:, x * 128 : (x + 1) * 128],
                sems.at[x],
            )
        )
        copies[x].start()
    contexts, blocks = [], []
    for i in range(2):
        mixed, _, mass = merge(arrived, i)
        done = (mixed / mass).astype(BF)
        mine = (iota((8, 128), 1) == z * 8 + iota((8, 128), 0)).astype(BF)
        contexts.append(dot(mine, done, ((1,), (1,))))
        tile = (iota((16, 256), 0) == iota((16, 256), 1) % 16).astype(BF)
        tiled = dot(done, tile, ((0,), (0,)))
        block = iota((128, 256), 0) // 8 == iota((128, 256), 1) // 16
        blocks.append(jnp.where(block, tiled, 0.0).astype(BF))
    context[...] = jnp.concatenate(contexts, axis=0).astype(BF)
    for copy in copies:
        copy.wait()
    terms = []
    for i in range(2):
        term = dot(blocks[i], weights[...], ((1,), (0,)))
        terms.append(jnp.sum(term.reshape(Z, 8, 512), axis=0))
    term = jnp.concatenate(terms, axis=0)
    tiles = [term[:, x * 128 : (x + 1) * 128] for x in range(X)]
    odd = (iota((B, 128), 0) * 0 + z) % 2 == 1
    parts = [
        jnp.where(odd, halves(first, second, 1), halves(first, second, 0))
        for first, second in (tiles[:2], tiles[2:])
    ]
    term = jnp.concatenate(parts, axis=1).astype(BF)
    for k in range(PLANE):
        out[k] = term


def slots(ids, expert, slot):
    hits = jnp.zeros(slot.shape, F32)
    for k in range(8):
        hits += (ids[k : k + 1, :] == expert).astype(F32)
    before = (iota((B, B), 0) < iota((B, B), 1)).astype(BF)
    rank = dot(hits.astype(BF), before, ((1,), (0,)))
    return (hits > 0.5) & (jnp.abs(rank - slot.astype(F32)) < 0.5)


def make_mid(arrived, hidden_cols, expert_ids, out, mid_part):
    x, _, cy = coordinates()
    projected = jnp.sum(arrived[...].astype(F32), axis=0)
    mid = (projected + hidden_cols[...]).astype(BF)
    row = iota((128, B), 0)
    table = slots(expert_ids[...], x * Z + row // 8, row % 4)
    picked = jnp.zeros((128, 128), F32)
    for t in range(2):
        half = (table & (row // 4 % 2 == t)).astype(BF)
        picked += dot(half, mid[:, t * 128 : (t + 1) * 128], ((1,), (0,)))
    out[...] = picked.reshape(Z, 8, 128).astype(BF)
    mine = iota((8, COLS), 1) == x * 64 + cy * 8 + iota((8, COLS), 0)
    mid_part[...] = dot(mine.astype(BF), mid, ((1,), (1,)))


def sort_columns(tiles):
    lane = iota((8, 128), 1)
    for bit in (32, 16, 8):
        low = lane // bit % 2 == 0
        high = lane // (2 * bit) % 2 == 0
        tiles = [
            jnp.where(
                low == high,
                tile,
                jnp.where(high, pltpu.roll(tile, 128 - bit, 1), pltpu.roll(tile, bit, 1)),
            )
            for tile in tiles
        ]
    for step in (4, 2, 1):
        low = lane // (16 * step) % 2 == 0
        swapped = list(tiles)
        for v in range(8):
            if v & step == 0:
                first, second = tiles[v], tiles[v + step]
                swapped[v] = jnp.where(low, first, pltpu.roll(second, 16 * step, 1))
                swapped[v + step] = jnp.where(low, pltpu.roll(first, 128 - 16 * step, 1), second)
        tiles = swapped
    return tiles


def experts(
    arrived, gain, expert_ids, route_weights, w_gate, w_up, w_down, out, held, sems
):
    copies = []
    for n, source in enumerate((w_gate, w_up, w_down)):
        for h in range(2):
            part = pl.ds(h * 64, 64)
            copies.append(
                pltpu.make_async_copy(source.at[part], held.at[n, part], sems.at[2 * n + h])
            )
    for copy in copies:
        copy.start()
    x, z, _ = coordinates()
    expert = x * Z + z
    ids = expert_ids[...]
    routes = route_weights[...]
    table = slots(ids, expert, iota((8, B), 0))
    share = routes / jnp.sum(routes, axis=0, keepdims=True)
    weight = jnp.sum(jnp.where(ids == expert, share, 0.0), axis=0, keepdims=True)
    coefficient = jnp.sum(jnp.where(table, weight, 0.0), axis=1, keepdims=True)
    first_half = iota((8, 128), 0) < 4
    gains = gain[...].astype(F32)
    tiles, scaled = [], []
    for p in range(2):
        for v in range(Z // 2):
            tile = halves(arrived[2 * v].astype(F32), arrived[2 * v + 1].astype(F32), p)
            low, high = p * 8 + v, (2 + p) * 8 + v
            tiles.append(tile * tile)
            scaled.append(
                tile * jnp.where(first_half, gains[low : low + 1], gains[high : high + 1])
            )
    squares = sum(tiles[1:], tiles[0])
    squares = squares + jnp.concatenate([squares[4:], squares[:4]], axis=0)
    scale = lax.rsqrt(jnp.sum(squares, axis=1, keepdims=True) * (1.0 / D) + 1e-06)
    picked = jnp.concatenate([(tile * scale).astype(BF) for tile in scaled], axis=1)

    def project(weights):
        near = dot(picked, weights[:, : D // 2], ((1,), (1,)))
        far = dot(picked, weights[:, D // 2 :], ((1,), (1,)))
        return near + jnp.concatenate([far[4:], far[:4]], axis=0)

    halves_of = [copies[2 * n : 2 * n + 2] for n in range(3)]
    for copy in halves_of[0]:
        copy.wait()
    gate = project(held.at[0])
    for copy in halves_of[1]:
        copy.wait()
    upward = project(held.at[1])
    hidden_units = (gate / (1.0 + jnp.exp(-gate)) * upward).astype(BF)
    for copy in halves_of[2]:
        copy.wait()
    weighted = dot(hidden_units, held[2], ((1,), (0,))) * coefficient
    for group in range(X):
        start = group * 1024
        tiles = [weighted[:, start + v * 128 : start + (v + 1) * 128] for v in range(8)]
        for c, tile in enumerate(sort_columns(tiles)):
            out[group * CY + c] = tile.astype(BF)


def sum_experts(arrived, expert_ids, out):
    z = lax.axis_index("z")
    parts = [
        jnp.sum(arrived[x * CY : (x + 1) * CY].astype(F32), axis=0) for x in range(X)
    ]
    row = iota((8 * X, B), 0)
    table = slots(expert_ids[...], row // 8 * Z + z, row % 8).astype(F32)
    turned = dot(jnp.concatenate(parts, axis=0), table, ((0,), (0,)), EXACT)
    out[...] = turned.reshape(Z, 8, B).astype(BF)


def finish_layer(arrived, mid_part, out):
    out[...] = (mid_part[...] + jnp.sum(arrived[...].astype(F32), axis=0)).astype(BF)


def call(body, outs, arrays, far=(), scratch=(), limit=16):
    vmem = pl.BlockSpec(memory_space=pltpu.VMEM)
    remote = pl.BlockSpec(memory_space=pltpu.HBM)
    single = not isinstance(outs, list)
    return pl.pallas_call(
        body,
        out_shape=outs,
        in_specs=[vmem] * len(arrays) + [remote] * len(far),
        out_specs=vmem if single else [vmem] * len(outs),
        scratch_shapes=list(scratch),
        compiler_params=pltpu.CompilerParams(vmem_limit_bytes=limit * 1024 * 1024),
    )(*arrays, *far)


def swap(blocks, axes):
    return lax.all_to_all(blocks, axes, 0, 0, tiled=True)


def shards(
    query,
    key_cache,
    value_cache,
    lengths,
    hidden_in,
    out_proj,
    norm_gain,
    expert_ids,
    route_weights,
    w_gate,
    w_up,
    w_down,
):
    ids, routes = expert_ids.T, route_weights.T
    dma, vmem = pltpu.SemaphoreType.DMA, pltpu.VMEM

    def shape(*dims, dtype=BF):
        return jax.ShapeDtypeStruct(dims, dtype)

    rows = lax.all_gather(out_proj, "z", axis=0, tiled=True)
    packed, limits = call(
        pack_query,
        [shape(Z, 8, 128), shape(B, 128, dtype=jnp.int32)],
        (),
        (query, lengths),
        (vmem((B, 16), BF), pltpu.SMEM((B,), jnp.int32), dma((2,))),
        62,
    )
    spread = call(spread_query, shape(PLANE, 32, 128), (swap(packed, "z"),))
    cache = vmem((B, SPAN, 512), BF)
    partial = call(
        attend,
        shape(PLANE, 40, 128),
        (swap(spread, PLANE_AXES),),
        (key_cache, value_cache, hidden_in.T, limits),
        (cache, cache, vmem((8, B), BF), vmem((B, 128), jnp.int32), dma((6,))),
        62,
    )
    merged, hidden_cols = call(
        merge_plane,
        [shape(Z, 40, 128), shape(B, COLS, dtype=F32)],
        (swap(partial, PLANE_AXES),),
    )
    context, term = call(
        finish_context,
        [shape(B, 16), shape(PLANE, B, COLS)],
        (swap(merged, "z"),),
        (rows,),
        (vmem((Z * 16, 512), BF), dma((X,))),
        62,
    )
    picked, mid_part = call(
        make_mid,
        [shape(Z, 8, 128), shape(8, B, dtype=F32)],
        (swap(term, PLANE_AXES), hidden_cols, ids),
    )
    mixture = call(
        experts,
        shape(PLANE, 8, 128),
        (swap(picked, "z"), norm_gain.reshape(PLANE, 128), ids, routes),
        (w_gate, w_up, w_down),
        (vmem((3, 128, D), BF), dma((6,))),
        62,
    )
    summed = call(sum_experts, shape(Z, 8, B), (swap(mixture, PLANE_AXES), ids))
    layer_out = call(finish_layer, shape(8, B), (swap(summed, "z"), mid_part))
    return context, layer_out.T


def solution(mesh):
    fine = Mesh(np.asarray(mesh.devices).reshape(X, Z, 2, 4), ALL_AXES)
    columns, rows = P(None, ALL_AXES), P(ALL_AXES, None)
    cache = P(None, ALL_AXES, None)
    placed = (
        columns,
        cache,
        cache,
        P(),
        columns,
        rows,
        P(),
        P(),
        P(),
        rows,
        rows,
        rows,
    )
    return jax.shard_map(
        shards,
        mesh=fine,
        in_specs=placed,
        out_specs=(columns, columns),
        check_vma=False,
    )
```

```python
import math

import jax
import jax.numpy as jnp
import numpy as np
from jax import lax
from jax.experimental import pallas as pl
from jax.experimental.pallas import tpu as pltpu
from jax.sharding import Mesh
from jax.sharding import PartitionSpec as P

HD = 128
X, Z, CY = 4, 16, 8
PLANE = X * CY
B = 16
D = 4096
COLS = D // Z
SPAN = 32
FLOOR = -1e30
BF = jnp.bfloat16
F32 = jnp.float32
PLANE_AXES = ("x", "c", "y")
ALL_AXES = ("x", "z", "c", "y")
EXACT = lax.Precision.HIGHEST


def iota(shape, dimension):
    return lax.broadcasted_iota(jnp.int32, shape, dimension)


def dot(a, b, dims, precision=None):
    return lax.dot_general(
        a, b, (dims, ((), ())), preferred_element_type=F32, precision=precision
    )


def eye(n, dtype=BF):
    return (iota((n, n), 0) == iota((n, n), 1)).astype(dtype)


def halves(first, second, high):
    low_lanes = iota(first.shape, 1) < 64
    if high:
        return jnp.where(low_lanes, pltpu.roll(first, 64, 1), second)
    return jnp.where(low_lanes, first, pltpu.roll(second, 64, 1))


def coordinates():
    x, z = lax.axis_index("x"), lax.axis_index("z")
    return x, z, lax.axis_index("c") * 4 + lax.axis_index("y")


def deal_out(query, out_proj, out, held_query, held, sems):
    copies = [
        pltpu.make_async_copy(query, held_query, sems.at[0]),
        pltpu.make_async_copy(out_proj, held, sems.at[1]),
    ]
    for copy in copies:
        copy.start()
    copies[0].wait()
    own = held_query[...]
    parts = []
    for i in range(2):
        put = (iota((16, 128), 0) + i * 16 == iota((16, 128), 1)).astype(BF)
        parts.append(dot(own, put, ((1,), (0,)))[i * 8 : (i + 1) * 8])
    wide = (parts[0] + parts[1]).astype(BF)
    copies[1].wait()
    for v in range(Z // 2):
        tiles = [
            held[:, x * 1024 + v * 128 : x * 1024 + (v + 1) * 128] for x in range(X)
        ]
        for high in range(2):
            pieces = [halves(tiles[0], tiles[1], high), halves(tiles[2], tiles[3], high), wide]
            out[2 * v + high] = jnp.concatenate(pieces, axis=0)


def spread_query(arrived, lengths, hidden, out, rows_out):
    rows = arrived[:, 32:40, :].astype(F32).reshape(128, 128).astype(BF)
    turned = dot(rows, eye(128), ((0,), (0,)))[:32].astype(BF)
    for k in range(PLANE):
        out[k] = turned
    own = iota((B, B), 0) == iota((B, B), 1)
    column = jnp.sum(jnp.where(own, lengths[...].astype(F32), 0.0), axis=1, keepdims=True)
    rows_out[0:B] = jnp.broadcast_to(column, (B, 128))
    spot = (iota((B, 128), 0) == iota((B, 128), 1) % B).astype(BF)
    repeated = dot(hidden[...], spot, ((1,), (0,)))
    own = jnp.where(iota((8, 128), 0) == iota((8, 128), 1) // B, repeated, 0.0)
    rows_out[B : B + 8] = jnp.broadcast_to(jnp.sum(own, axis=0, keepdims=True), (8, 128))


def attend(gathered, keys, values, extra, out):
    x, z, cy = coordinates()
    device = (x * Z + z) * CY + cy
    lane_j = iota((SPAN, 128), 1) % 8
    position = device * SPAN + iota((SPAN, 128), 0)
    own = extra[B : B + 1]
    zero = jnp.zeros((1, 128), F32)
    position = position.astype(F32)
    limit = extra[0:B]
    valids = []
    for i in range(2):
        rows = [
            (lane_j == j) & (position < limit[i * 8 + j : i * 8 + j + 1]) for j in range(8)
        ]
        valids.append(jnp.concatenate([r.astype(F32) for r in rows], axis=0) > 0.5)
    for g in range(X):
        parts, tops, highs, lows = [], [], [], []
        for i in range(2):
            query = gathered[g * CY : (g + 1) * CY, i * 16 : (i + 1) * 16, :].reshape(HD, 128)
            k = keys[i * 8 : (i + 1) * 8, :, g * HD : (g + 1) * HD].reshape(8 * SPAN, HD)
            v = values[i * 8 : (i + 1) * 8, :, g * HD : (g + 1) * HD].reshape(8 * SPAN, HD)
            scores = dot(k, query, ((1,), (0,))) * (1.0 / math.sqrt(HD))
            scores = jnp.where(valids[i], scores, FLOOR)
            top = jnp.max(scores, axis=0, keepdims=True).astype(BF).astype(F32)
            weights = jnp.where(valids[i], jnp.exp(scores - top), 0.0).astype(BF)
            total = jnp.sum(weights.astype(F32), axis=0, keepdims=True)
            high = total.astype(BF).astype(F32)
            parts.append(dot(v, weights, ((0,), (0,))))
            tops.append(top)
            highs.append(high)
            lows.append(total - high)
        block = jnp.concatenate(tops + highs + lows + [own, zero], axis=0)
        for c in range(CY):
            pieces = [part[c * 16 : (c + 1) * 16] for part in parts]
            out[g * CY + c] = jnp.concatenate(pieces + [block], axis=0).astype(BF)


def merge(arrived, i):
    top = arrived[:, 32 + i, :].astype(F32)
    total = arrived[:, 34 + i, :].astype(F32) + arrived[:, 36 + i, :].astype(F32)
    best = jnp.max(top, axis=0, keepdims=True)
    scale = jnp.exp(top - best)
    mass = jnp.sum(total * scale, axis=0, keepdims=True)
    mixed = arrived[:, i * 16 : (i + 1) * 16, :].astype(F32)
    return jnp.sum(mixed * scale[:, None, :], axis=0), best, mass


def merge_plane(arrived, out, hidden_cols):
    parts, tops, highs, lows = [], [], [], []
    for i in range(2):
        mixed, best, mass = merge(arrived, i)
        high = mass.astype(BF).astype(F32)
        parts.append(mixed)
        tops.append(best)
        highs.append(high)
        lows.append(mass - high)
    full = jnp.concatenate(
        parts + tops + highs + lows + [jnp.zeros((2, 128), F32)], axis=0
    ).astype(BF)
    for z in range(Z):
        out[z] = full
    owned = arrived[:, 38, :].astype(F32).astype(BF)
    for t in range(2):
        put = (iota((16, 128), 0) == iota((16, 128), 1) // 8).astype(BF)
        by_lane = dot(owned[t * 16 : (t + 1) * 16], put, ((0,), (0,)))
        mine = iota((128, 128), 0) // B == iota((128, 128), 1) % 8
        by_lane = jnp.where(mine, by_lane, 0.0).reshape(8, B, 128)
        hidden_cols[:, t * 128 : (t + 1) * 128] = jnp.sum(by_lane, axis=0)


def finish_context(arrived, dealt, context, out):
    z = lax.axis_index("z")
    weights = jnp.concatenate(
        [dealt[:, t * 16 : (t + 1) * 16, :].reshape(Z * 16, 128) for t in range(2)], axis=1
    )
    contexts, terms = [], []
    for i in range(2):
        mixed, _, mass = merge(arrived, i)
        done = (mixed / mass).astype(BF)
        mine = (iota((8, 128), 1) == z * 8 + iota((8, 128), 0)).astype(BF)
        contexts.append(dot(mine, done, ((1,), (1,))))
        tile = (iota((16, 256), 0) == iota((16, 256), 1) % 16).astype(BF)
        tiled = dot(done, tile, ((0,), (0,)))
        block = iota((128, 256), 0) // 8 == iota((128, 256), 1) // 16
        tiled = jnp.where(block, tiled, 0.0).astype(BF)
        term = dot(tiled, weights, ((1,), (0,)))
        terms.append(jnp.sum(term.reshape(Z, 8, COLS), axis=0))
    context[...] = jnp.concatenate(contexts, axis=0).astype(BF)
    term = jnp.concatenate(terms, axis=0).astype(BF)
    for k in range(PLANE):
        out[k] = term


def slots(ids, expert, slot):
    hits = jnp.zeros(slot.shape, F32)
    for k in range(8):
        hits += (ids[k : k + 1, :] == expert).astype(F32)
    before = (iota((B, B), 0) < iota((B, B), 1)).astype(BF)
    rank = dot(hits.astype(BF), before, ((1,), (0,)))
    return (hits > 0.5) & (jnp.abs(rank - slot.astype(F32)) < 0.5)


def make_mid(arrived, hidden_cols, expert_ids, out, mid_part):
    x, _, cy = coordinates()
    projected = jnp.sum(arrived[...].astype(F32), axis=0)
    mid = (projected + hidden_cols[...]).astype(BF)
    row = iota((128, B), 0)
    table = slots(expert_ids[...], x * Z + row // 8, row % 4)
    picked = jnp.zeros((128, 128), F32)
    for t in range(2):
        half = (table & (row // 4 % 2 == t)).astype(BF)
        picked += dot(half, mid[:, t * 128 : (t + 1) * 128], ((1,), (0,)))
    out[...] = picked.reshape(Z, 8, 128).astype(BF)
    mine = iota((8, COLS), 1) == x * 64 + cy * 8 + iota((8, COLS), 0)
    mid_part[...] = dot(mine.astype(BF), mid, ((1,), (1,)))


def sort_columns(tiles):
    lane = iota((8, 128), 1)
    for bit in (32, 16, 8):
        low = lane // bit % 2 == 0
        high = lane // (2 * bit) % 2 == 0
        tiles = [
            jnp.where(
                low == high,
                tile,
                jnp.where(high, pltpu.roll(tile, 128 - bit, 1), pltpu.roll(tile, bit, 1)),
            )
            for tile in tiles
        ]
    for step in (4, 2, 1):
        low = lane // (16 * step) % 2 == 0
        swapped = list(tiles)
        for v in range(8):
            if v & step == 0:
                first, second = tiles[v], tiles[v + step]
                swapped[v] = jnp.where(low, first, pltpu.roll(second, 16 * step, 1))
                swapped[v + step] = jnp.where(low, pltpu.roll(first, 128 - 16 * step, 1), second)
        tiles = swapped
    return tiles


def experts(arrived, gain, expert_ids, route_weights, w_gate, w_up, w_down, out):
    x, z, _ = coordinates()
    expert = x * Z + z
    ids = expert_ids[...]
    routes = route_weights[...]
    table = slots(ids, expert, iota((8, B), 0))
    share = routes / jnp.sum(routes, axis=0, keepdims=True)
    weight = jnp.sum(jnp.where(ids == expert, share, 0.0), axis=0, keepdims=True)
    coefficient = jnp.sum(jnp.where(table, weight, 0.0), axis=1, keepdims=True)
    first_half = iota((8, 128), 0) < 4
    gains = gain[...].astype(F32)
    tiles, scaled = [], []
    for p in range(2):
        for v in range(Z // 2):
            tile = halves(arrived[2 * v].astype(F32), arrived[2 * v + 1].astype(F32), p)
            low, high = p * 8 + v, (2 + p) * 8 + v
            tiles.append(tile * tile)
            scaled.append(
                tile * jnp.where(first_half, gains[low : low + 1], gains[high : high + 1])
            )
    squares = sum(tiles[1:], tiles[0])
    squares = squares + jnp.concatenate([squares[4:], squares[:4]], axis=0)
    scale = lax.rsqrt(jnp.sum(squares, axis=1, keepdims=True) * (1.0 / D) + 1e-06)
    picked = jnp.concatenate([(tile * scale).astype(BF) for tile in scaled], axis=1)

    def project(weights):
        near = dot(picked, weights[:, : D // 2], ((1,), (1,)))
        far = dot(picked, weights[:, D // 2 :], ((1,), (1,)))
        return near + jnp.concatenate([far[4:], far[:4]], axis=0)

    gate = project(w_gate)
    upward = project(w_up)
    hidden_units = (gate / (1.0 + jnp.exp(-gate)) * upward).astype(BF)
    weighted = dot(hidden_units, w_down[...], ((1,), (0,))) * coefficient
    for group in range(X):
        start = group * 1024
        tiles = [weighted[:, start + v * 128 : start + (v + 1) * 128] for v in range(8)]
        for c, tile in enumerate(sort_columns(tiles)):
            out[group * CY + c] = tile.astype(BF)


def sum_experts(arrived, expert_ids, out):
    z = lax.axis_index("z")
    parts = [
        jnp.sum(arrived[x * CY : (x + 1) * CY].astype(F32), axis=0) for x in range(X)
    ]
    row = iota((8 * X, B), 0)
    table = slots(expert_ids[...], row // 8 * Z + z, row % 8).astype(F32)
    turned = dot(jnp.concatenate(parts, axis=0), table, ((0,), (0,)), EXACT)
    out[...] = turned.reshape(Z, 8, B).astype(BF)


def finish_layer(arrived, mid_part, out):
    out[...] = (mid_part[...] + jnp.sum(arrived[...].astype(F32), axis=0)).astype(BF)


def call(body, outs, arrays, far=(), scratch=(), limit=16):
    vmem = pl.BlockSpec(memory_space=pltpu.VMEM)
    remote = pl.BlockSpec(memory_space=pltpu.HBM)
    single = not isinstance(outs, list)
    return pl.pallas_call(
        body,
        out_shape=outs,
        in_specs=[vmem] * len(arrays) + [remote] * len(far),
        out_specs=vmem if single else [vmem] * len(outs),
        scratch_shapes=list(scratch),
        compiler_params=pltpu.CompilerParams(vmem_limit_bytes=limit * 1024 * 1024),
    )(*arrays, *far)


def swap(blocks, axes):
    return lax.all_to_all(blocks, axes, 0, 0, tiled=True)


def shards(
    query,
    key_cache,
    value_cache,
    lengths,
    hidden_in,
    out_proj,
    norm_gain,
    expert_ids,
    route_weights,
    w_gate,
    w_up,
    w_down,
):
    ids, routes = expert_ids.T, route_weights.T
    dma, vmem = pltpu.SemaphoreType.DMA, pltpu.VMEM

    def shape(*dims, dtype=BF):
        return jax.ShapeDtypeStruct(dims, dtype)

    dealt = swap(
        call(
            deal_out,
            shape(Z, 40, 128),
            (),
            (query, out_proj),
            (vmem((B, 16), BF), vmem((16, D), BF), dma((2,))),
            62,
        ),
        "z",
    )
    spread, extra = call(
        spread_query,
        [shape(PLANE, 32, 128), shape(B + 8, 128, dtype=F32)],
        (dealt, lengths.reshape(1, B), hidden_in.T),
    )
    partial = call(
        attend,
        shape(PLANE, 40, 128),
        (swap(spread, PLANE_AXES), key_cache, value_cache, extra),
    )
    merged, hidden_cols = call(
        merge_plane,
        [shape(Z, 40, 128), shape(B, COLS, dtype=F32)],
        (swap(partial, PLANE_AXES),),
    )
    context, term = call(
        finish_context,
        [shape(B, 16), shape(PLANE, B, COLS)],
        (swap(merged, "z"), dealt),
    )
    picked, mid_part = call(
        make_mid,
        [shape(Z, 8, 128), shape(8, B, dtype=F32)],
        (swap(term, PLANE_AXES), hidden_cols, ids),
    )
    mixture = call(
        experts,
        shape(PLANE, 8, 128),
        (swap(picked, "z"), norm_gain.reshape(PLANE, 128), ids, routes, w_gate, w_up, w_down),
    )
    summed = call(sum_experts, shape(Z, 8, B), (swap(mixture, PLANE_AXES), ids))
    layer_out = call(finish_layer, shape(8, B), (swap(summed, "z"), mid_part))
    return context, layer_out.T


def solution(mesh):
    fine = Mesh(np.asarray(mesh.devices).reshape(X, Z, 2, 4), ALL_AXES)
    columns, rows = P(None, ALL_AXES), P(ALL_AXES, None)
    cache = P(None, ALL_AXES, None)
    placed = (
        columns,
        cache,
        cache,
        P(),
        columns,
        rows,
        P(),
        P(),
        P(),
        rows,
        rows,
        rows,
    )
    return jax.shard_map(
        shards,
        mesh=fine,
        in_specs=placed,
        out_specs=(columns, columns),
        check_vma=False,
    )
```

```python
import math

import jax
import jax.numpy as jnp
import numpy as np
from jax import lax
from jax.experimental import pallas as pl
from jax.experimental.pallas import tpu as pltpu
from jax.sharding import Mesh
from jax.sharding import PartitionSpec as P

HD = 128
X, Z, CY = 4, 16, 8
PLANE = X * CY
B = 16
D = 4096
COLS = D // Z
SPAN = 32
FLOOR = -1e30
BF = jnp.bfloat16
F32 = jnp.float32
PLANE_AXES = ("x", "c", "y")
ALL_AXES = ("x", "z", "c", "y")
EXACT = lax.Precision.HIGHEST


def iota(shape, dimension):
    return lax.broadcasted_iota(jnp.int32, shape, dimension)


def dot(a, b, dims, precision=None):
    return lax.dot_general(
        a, b, (dims, ((), ())), preferred_element_type=F32, precision=precision
    )


def eye(n, dtype=BF):
    return (iota((n, n), 0) == iota((n, n), 1)).astype(dtype)


def halves(first, second, high):
    low_lanes = iota(first.shape, 1) < 64
    if high:
        return jnp.where(low_lanes, pltpu.roll(first, 64, 1), second)
    return jnp.where(low_lanes, first, pltpu.roll(second, 64, 1))


def coordinates():
    x, z = lax.axis_index("x"), lax.axis_index("z")
    return x, z, lax.axis_index("c") * 4 + lax.axis_index("y")


def deal_out(query, out_proj, out, held_query, held, sems):
    copies = [
        pltpu.make_async_copy(query, held_query, sems.at[0]),
        pltpu.make_async_copy(out_proj, held, sems.at[1]),
    ]
    for copy in copies:
        copy.start()
    copies[0].wait()
    own = held_query[...]
    parts = []
    for i in range(2):
        put = (iota((16, 128), 0) + i * 16 == iota((16, 128), 1)).astype(BF)
        parts.append(dot(own, put, ((1,), (0,)))[i * 8 : (i + 1) * 8])
    wide = (parts[0] + parts[1]).astype(BF)
    copies[1].wait()
    for v in range(Z // 2):
        tiles = [
            held[:, x * 1024 + v * 128 : x * 1024 + (v + 1) * 128] for x in range(X)
        ]
        for high in range(2):
            pieces = [halves(tiles[0], tiles[1], high), halves(tiles[2], tiles[3], high), wide]
            out[2 * v + high] = jnp.concatenate(pieces, axis=0)


def spread_query(arrived, lengths, hidden, out, rows_out):
    rows = arrived[:, 32:40, :].astype(F32).reshape(128, 128).astype(BF)
    turned = dot(rows, eye(128), ((0,), (0,)))[:32].astype(BF)
    for k in range(PLANE):
        out[k] = turned
    own = iota((B, B), 0) == iota((B, B), 1)
    column = jnp.sum(jnp.where(own, lengths[...].astype(F32), 0.0), axis=1, keepdims=True)
    rows_out[0:B] = jnp.broadcast_to(column, (B, 128))
    spot = (iota((B, 128), 0) == iota((B, 128), 1) % B).astype(BF)
    repeated = dot(hidden[...], spot, ((1,), (0,)))
    own = jnp.where(iota((8, 128), 0) == iota((8, 128), 1) // B, repeated, 0.0)
    rows_out[B : B + 8] = jnp.broadcast_to(jnp.sum(own, axis=0, keepdims=True), (8, 128))


def attend(gathered, keys, values, extra, out):
    x, z, cy = coordinates()
    device = (x * Z + z) * CY + cy
    lane_j = iota((SPAN, 128), 1) % 8
    position = device * SPAN + iota((SPAN, 128), 0)
    own = extra[B : B + 1]
    zero = jnp.zeros((1, 128), F32)
    position = position.astype(F32)
    limit = extra[0:B]
    valids = []
    for i in range(2):
        rows = [
            (lane_j == j) & (position < limit[i * 8 + j : i * 8 + j + 1]) for j in range(8)
        ]
        valids.append(jnp.concatenate([r.astype(F32) for r in rows], axis=0) > 0.5)
    for g in range(X):
        parts, tops, highs, lows = [], [], [], []
        for i in range(2):
            query = gathered[g * CY : (g + 1) * CY, i * 16 : (i + 1) * 16, :].reshape(HD, 128)
            k = keys[i * 8 : (i + 1) * 8, :, g * HD : (g + 1) * HD].reshape(8 * SPAN, HD)
            v = values[i * 8 : (i + 1) * 8, :, g * HD : (g + 1) * HD].reshape(8 * SPAN, HD)
            scores = dot(k, query, ((1,), (0,))) * (1.0 / math.sqrt(HD))
            scores = jnp.where(valids[i], scores, FLOOR)
            top = jnp.max(scores, axis=0, keepdims=True).astype(BF).astype(F32)
            weights = jnp.where(valids[i], jnp.exp(scores - top), 0.0).astype(BF)
            total = jnp.sum(weights.astype(F32), axis=0, keepdims=True)
            high = total.astype(BF).astype(F32)
            parts.append(dot(v, weights, ((0,), (0,))))
            tops.append(top)
            highs.append(high)
            lows.append(total - high)
        block = jnp.concatenate(tops + highs + lows + [own, zero], axis=0)
        for c in range(CY):
            pieces = [part[c * 16 : (c + 1) * 16] for part in parts]
            out[g * CY + c] = jnp.concatenate(pieces + [block], axis=0).astype(BF)


def merge(arrived, i):
    top = arrived[:, 32 + i, :].astype(F32)
    total = arrived[:, 34 + i, :].astype(F32) + arrived[:, 36 + i, :].astype(F32)
    best = jnp.max(top, axis=0, keepdims=True)
    scale = jnp.exp(top - best)
    mass = jnp.sum(total * scale, axis=0, keepdims=True)
    mixed = arrived[:, i * 16 : (i + 1) * 16, :].astype(F32)
    return jnp.sum(mixed * scale[:, None, :], axis=0), best, mass


def merge_plane(arrived, out, hidden_cols):
    parts, tops, highs, lows = [], [], [], []
    for i in range(2):
        mixed, best, mass = merge(arrived, i)
        high = mass.astype(BF).astype(F32)
        parts.append(mixed)
        tops.append(best)
        highs.append(high)
        lows.append(mass - high)
    full = jnp.concatenate(
        parts + tops + highs + lows + [jnp.zeros((2, 128), F32)], axis=0
    ).astype(BF)
    for z in range(Z):
        out[z] = full
    owned = arrived[:, 38, :].astype(F32).astype(BF)
    for t in range(2):
        put = (iota((16, 128), 0) == iota((16, 128), 1) // 8).astype(BF)
        by_lane = dot(owned[t * 16 : (t + 1) * 16], put, ((0,), (0,)))
        mine = iota((128, 128), 0) // B == iota((128, 128), 1) % 8
        by_lane = jnp.where(mine, by_lane, 0.0).reshape(8, B, 128)
        hidden_cols[:, t * 128 : (t + 1) * 128] = jnp.sum(by_lane, axis=0)


def finish_context(arrived, dealt, context, out):
    z = lax.axis_index("z")
    weights = jnp.concatenate(
        [dealt[:, t * 16 : (t + 1) * 16, :].reshape(Z * 16, 128) for t in range(2)], axis=1
    )
    contexts, terms = [], []
    for i in range(2):
        mixed, _, mass = merge(arrived, i)
        done = (mixed / mass).astype(BF)
        mine = (iota((8, 128), 1) == z * 8 + iota((8, 128), 0)).astype(BF)
        contexts.append(dot(mine, done, ((1,), (1,))))
        tile = (iota((16, 256), 0) == iota((16, 256), 1) % 16).astype(BF)
        tiled = dot(done, tile, ((0,), (0,)))
        block = iota((128, 256), 0) // 8 == iota((128, 256), 1) // 16
        tiled = jnp.where(block, tiled, 0.0).astype(BF)
        term = dot(tiled, weights, ((1,), (0,)))
        terms.append(jnp.sum(term.reshape(Z, 8, COLS), axis=0))
    context[...] = jnp.concatenate(contexts, axis=0).astype(BF)
    term = jnp.concatenate(terms, axis=0).astype(BF)
    for k in range(PLANE):
        out[k] = term


def slots(ids, expert, slot):
    hits = jnp.zeros(slot.shape, F32)
    for k in range(8):
        hits += (ids[k : k + 1, :] == expert).astype(F32)
    before = (iota((B, B), 0) < iota((B, B), 1)).astype(BF)
    rank = dot(hits.astype(BF), before, ((1,), (0,)))
    return (hits > 0.5) & (jnp.abs(rank - slot.astype(F32)) < 0.5)


def make_mid(arrived, hidden_cols, expert_ids, out, mid_part):
    x, _, cy = coordinates()
    projected = jnp.sum(arrived[...].astype(F32), axis=0)
    mid = (projected + hidden_cols[...]).astype(BF)
    row = iota((128, B), 0)
    table = slots(expert_ids[...], x * Z + row // 8, row % 4)
    picked = jnp.zeros((128, 128), F32)
    for t in range(2):
        half = (table & (row // 4 % 2 == t)).astype(BF)
        picked += dot(half, mid[:, t * 128 : (t + 1) * 128], ((1,), (0,)))
    out[...] = picked.reshape(Z, 8, 128).astype(BF)
    mine = iota((8, COLS), 1) == x * 64 + cy * 8 + iota((8, COLS), 0)
    mid_part[...] = dot(mine.astype(BF), mid, ((1,), (1,)))


def sort_columns(tiles):
    lane = iota((8, 128), 1)
    for bit in (32, 16, 8):
        low = lane // bit % 2 == 0
        high = lane // (2 * bit) % 2 == 0
        tiles = [
            jnp.where(
                low == high,
                tile,
                jnp.where(high, pltpu.roll(tile, 128 - bit, 1), pltpu.roll(tile, bit, 1)),
            )
            for tile in tiles
        ]
    for step in (4, 2, 1):
        low = lane // (16 * step) % 2 == 0
        swapped = list(tiles)
        for v in range(8):
            if v & step == 0:
                first, second = tiles[v], tiles[v + step]
                swapped[v] = jnp.where(low, first, pltpu.roll(second, 16 * step, 1))
                swapped[v + step] = jnp.where(low, pltpu.roll(first, 128 - 16 * step, 1), second)
        tiles = swapped
    return tiles


def experts(arrived, gain, expert_ids, route_weights, w_gate, w_up, w_down, out):
    x, z, _ = coordinates()
    expert = x * Z + z
    ids = expert_ids[...]
    routes = route_weights[...]
    table = slots(ids, expert, iota((8, B), 0))
    share = routes / jnp.sum(routes, axis=0, keepdims=True)
    weight = jnp.sum(jnp.where(ids == expert, share, 0.0), axis=0, keepdims=True)
    coefficient = jnp.sum(jnp.where(table, weight, 0.0), axis=1, keepdims=True)
    first_half = iota((8, 128), 0) < 4
    gains = gain[...].astype(F32)
    tiles, scaled = [], []
    for p in range(2):
        for v in range(Z // 2):
            tile = halves(arrived[2 * v].astype(F32), arrived[2 * v + 1].astype(F32), p)
            low, high = p * 8 + v, (2 + p) * 8 + v
            tiles.append(tile * tile)
            scaled.append(
                tile * jnp.where(first_half, gains[low : low + 1], gains[high : high + 1])
            )
    squares = sum(tiles[1:], tiles[0])
    squares = squares + jnp.concatenate([squares[4:], squares[:4]], axis=0)
    scale = lax.rsqrt(jnp.sum(squares, axis=1, keepdims=True) * (1.0 / D) + 1e-06)
    picked = jnp.concatenate([(tile * scale).astype(BF) for tile in scaled], axis=1)

    def project(weights):
        near = dot(picked, weights[:, : D // 2], ((1,), (1,)))
        far = dot(picked, weights[:, D // 2 :], ((1,), (1,)))
        return near + jnp.concatenate([far[4:], far[:4]], axis=0)

    gate = project(w_gate)
    upward = project(w_up)
    hidden_units = (gate / (1.0 + jnp.exp(-gate)) * upward).astype(BF)
    weighted = dot(hidden_units, w_down[...], ((1,), (0,))) * coefficient
    for group in range(X):
        start = group * 1024
        tiles = [weighted[:, start + v * 128 : start + (v + 1) * 128] for v in range(8)]
        for c, tile in enumerate(sort_columns(tiles)):
            out[group * CY + c] = tile[:4].astype(BF)


def sum_experts(arrived, expert_ids, out):
    z = lax.axis_index("z")
    parts = [
        jnp.sum(arrived[x * CY : (x + 1) * CY].astype(F32), axis=0) for x in range(X)
    ]
    row = iota((4 * X, B), 0)
    table = slots(expert_ids[...], row // 4 * Z + z, row % 4).astype(F32)
    turned = dot(jnp.concatenate(parts, axis=0), table, ((0,), (0,)), EXACT).astype(BF)
    spot = (iota((B, 128), 0) == iota((B, 128), 1) % B).astype(BF)
    wide = dot(turned, spot, ((1,), (0,)))
    wide = jnp.where(iota((128, 128), 0) % 8 == iota((128, 128), 1) // B, wide, 0.0)
    rows = jnp.sum(wide.reshape(Z, 8, 128), axis=1, keepdims=True)
    out[...] = rows.astype(BF)


def finish_layer(arrived, mid_part, out):
    total = jnp.sum(arrived[...].astype(F32), axis=0)
    wide = jnp.where(iota((8, 128), 0) == iota((8, 128), 1) // B, total, 0.0)
    fold = (iota((128, B), 0) % B == iota((128, B), 1)).astype(F32)
    mixture = dot(wide, fold, ((1,), (0,)), EXACT)
    out[...] = (mid_part[...] + mixture).astype(BF)


def call(body, outs, arrays, far=(), scratch=(), limit=16):
    vmem = pl.BlockSpec(memory_space=pltpu.VMEM)
    remote = pl.BlockSpec(memory_space=pltpu.HBM)
    single = not isinstance(outs, list)
    return pl.pallas_call(
        body,
        out_shape=outs,
        in_specs=[vmem] * len(arrays) + [remote] * len(far),
        out_specs=vmem if single else [vmem] * len(outs),
        scratch_shapes=list(scratch),
        compiler_params=pltpu.CompilerParams(vmem_limit_bytes=limit * 1024 * 1024),
    )(*arrays, *far)


def swap(blocks, axes):
    return lax.all_to_all(blocks, axes, 0, 0, tiled=True)


def shards(
    query,
    key_cache,
    value_cache,
    lengths,
    hidden_in,
    out_proj,
    norm_gain,
    expert_ids,
    route_weights,
    w_gate,
    w_up,
    w_down,
):
    ids, routes = expert_ids.T, route_weights.T
    dma, vmem = pltpu.SemaphoreType.DMA, pltpu.VMEM

    def shape(*dims, dtype=BF):
        return jax.ShapeDtypeStruct(dims, dtype)

    dealt = swap(
        call(
            deal_out,
            shape(Z, 40, 128),
            (),
            (query, out_proj),
            (vmem((B, 16), BF), vmem((16, D), BF), dma((2,))),
            62,
        ),
        "z",
    )
    spread, extra = call(
        spread_query,
        [shape(PLANE, 32, 128), shape(B + 8, 128, dtype=F32)],
        (dealt, lengths.reshape(1, B), hidden_in.T),
    )
    partial = call(
        attend,
        shape(PLANE, 40, 128),
        (swap(spread, PLANE_AXES), key_cache, value_cache, extra),
    )
    merged, hidden_cols = call(
        merge_plane,
        [shape(Z, 40, 128), shape(B, COLS, dtype=F32)],
        (swap(partial, PLANE_AXES),),
    )
    context, term = call(
        finish_context,
        [shape(B, 16), shape(PLANE, B, COLS)],
        (swap(merged, "z"), dealt),
    )
    picked, mid_part = call(
        make_mid,
        [shape(Z, 8, 128), shape(8, B, dtype=F32)],
        (swap(term, PLANE_AXES), hidden_cols, ids),
    )
    mixture = call(
        experts,
        shape(PLANE, 4, 128),
        (swap(picked, "z"), norm_gain.reshape(PLANE, 128), ids, routes, w_gate, w_up, w_down),
    )
    summed = call(sum_experts, shape(Z, 1, 128), (swap(mixture, PLANE_AXES), ids))
    layer_out = call(finish_layer, shape(8, B), (swap(summed, "z"), mid_part))
    return context, layer_out.T


def solution(mesh):
    fine = Mesh(np.asarray(mesh.devices).reshape(X, Z, 2, 4), ALL_AXES)
    columns, rows = P(None, ALL_AXES), P(ALL_AXES, None)
    cache = P(None, ALL_AXES, None)
    placed = (
        columns,
        cache,
        cache,
        P(),
        columns,
        rows,
        P(),
        P(),
        P(),
        rows,
        rows,
        rows,
    )
    return jax.shard_map(
        shards,
        mesh=fine,
        in_specs=placed,
        out_specs=(columns, columns),
        check_vma=False,
    )
```

```python
import math

import jax
import jax.numpy as jnp
import numpy as np
from jax import lax
from jax.experimental import pallas as pl
from jax.experimental.pallas import tpu as pltpu
from jax.sharding import Mesh
from jax.sharding import PartitionSpec as P

HD = 128
X, Z, CY = 4, 16, 8
PLANE = X * CY
B = 16
D = 4096
COLS = D // Z
SPAN = 32
FLOOR = -1e30
BF = jnp.bfloat16
F32 = jnp.float32
PLANE_AXES = ("x", "c", "y")
ALL_AXES = ("x", "z", "c", "y")
EXACT = lax.Precision.HIGHEST


def iota(shape, dimension):
    return lax.broadcasted_iota(jnp.int32, shape, dimension)


def dot(a, b, dims, precision=None):
    return lax.dot_general(
        a, b, (dims, ((), ())), preferred_element_type=F32, precision=precision
    )


def eye(n, dtype=BF):
    return (iota((n, n), 0) == iota((n, n), 1)).astype(dtype)


def halves(first, second, high):
    low_lanes = iota(first.shape, 1) < 64
    if high:
        return jnp.where(low_lanes, pltpu.roll(first, 64, 1), second)
    return jnp.where(low_lanes, first, pltpu.roll(second, 64, 1))


def coordinates():
    x, z = lax.axis_index("x"), lax.axis_index("z")
    return x, z, lax.axis_index("c") * 4 + lax.axis_index("y")


def deal_out(query, out_proj, out, held_query, held, sems):
    copies = [
        pltpu.make_async_copy(query, held_query, sems.at[0]),
        pltpu.make_async_copy(out_proj, held, sems.at[1]),
    ]
    for copy in copies:
        copy.start()
    copies[0].wait()
    own = held_query[...]
    parts = []
    for i in range(2):
        put = (iota((16, 128), 0) + i * 16 == iota((16, 128), 1)).astype(BF)
        parts.append(dot(own, put, ((1,), (0,)))[i * 8 : (i + 1) * 8])
    wide = (parts[0] + parts[1]).astype(BF)
    copies[1].wait()
    for v in range(Z // 2):
        tiles = [
            held[:, x * 1024 + v * 128 : x * 1024 + (v + 1) * 128] for x in range(X)
        ]
        for high in range(2):
            pieces = [halves(tiles[0], tiles[1], high), halves(tiles[2], tiles[3], high), wide]
            out[2 * v + high] = jnp.concatenate(pieces, axis=0)


def spread_query(arrived, lengths, hidden, out, rows_out):
    rows = arrived[:, 32:40, :].astype(F32).reshape(128, 128).astype(BF)
    turned = dot(rows, eye(128), ((0,), (0,)))[:32].astype(BF)
    for k in range(PLANE):
        out[k] = turned
    own = iota((B, B), 0) == iota((B, B), 1)
    column = jnp.sum(jnp.where(own, lengths[...].astype(F32), 0.0), axis=1, keepdims=True)
    rows_out[0:B] = jnp.broadcast_to(column, (B, 128))
    spot = (iota((B, 128), 0) == iota((B, 128), 1) % B).astype(BF)
    repeated = dot(hidden[...], spot, ((1,), (0,)))
    own = jnp.where(iota((8, 128), 0) == iota((8, 128), 1) // B, repeated, 0.0)
    rows_out[B : B + 8] = jnp.broadcast_to(jnp.sum(own, axis=0, keepdims=True), (8, 128))


def attend(gathered, keys, values, extra, out):
    x, z, cy = coordinates()
    device = (x * Z + z) * CY + cy
    lane_j = iota((SPAN, 128), 1) % 8
    position = device * SPAN + iota((SPAN, 128), 0)
    own = extra[B : B + 1]
    zero = jnp.zeros((1, 128), F32)
    position = position.astype(F32)
    limit = extra[0:B]
    valids = []
    for i in range(2):
        rows = [
            (lane_j == j) & (position < limit[i * 8 + j : i * 8 + j + 1]) for j in range(8)
        ]
        valids.append(jnp.concatenate([r.astype(F32) for r in rows], axis=0) > 0.5)
    for g in range(X):
        parts, tops, highs, lows = [], [], [], []
        for i in range(2):
            query = gathered[g * CY : (g + 1) * CY, i * 16 : (i + 1) * 16, :].reshape(HD, 128)
            k = keys[i * 8 : (i + 1) * 8, :, g * HD : (g + 1) * HD].reshape(8 * SPAN, HD)
            v = values[i * 8 : (i + 1) * 8, :, g * HD : (g + 1) * HD].reshape(8 * SPAN, HD)
            scores = dot(k, query, ((1,), (0,))) * (1.0 / math.sqrt(HD))
            scores = jnp.where(valids[i], scores, FLOOR)
            top = jnp.max(scores, axis=0, keepdims=True).astype(BF).astype(F32)
            weights = jnp.where(valids[i], jnp.exp(scores - top), 0.0).astype(BF)
            total = jnp.sum(weights.astype(F32), axis=0, keepdims=True)
            high = total.astype(BF).astype(F32)
            parts.append(dot(v, weights, ((0,), (0,))))
            tops.append(top)
            highs.append(high)
            lows.append(total - high)
        block = jnp.concatenate(tops + highs + lows + [own, zero], axis=0)
        for c in range(CY):
            pieces = [part[c * 16 : (c + 1) * 16] for part in parts]
            out[g * CY + c] = jnp.concatenate(pieces + [block], axis=0).astype(BF)


def merge(arrived, i):
    top = arrived[:, 32 + i, :].astype(F32)
    total = arrived[:, 34 + i, :].astype(F32) + arrived[:, 36 + i, :].astype(F32)
    best = jnp.max(top, axis=0, keepdims=True)
    scale = jnp.exp(top - best)
    mass = jnp.sum(total * scale, axis=0, keepdims=True)
    mixed = arrived[:, i * 16 : (i + 1) * 16, :].astype(F32)
    return jnp.sum(mixed * scale[:, None, :], axis=0), best, mass


def merge_plane(arrived, out, hidden_cols):
    parts, tops, highs, lows = [], [], [], []
    for i in range(2):
        mixed, best, mass = merge(arrived, i)
        high = mass.astype(BF).astype(F32)
        parts.append(mixed)
        tops.append(best)
        highs.append(high)
        lows.append(mass - high)
    full = jnp.concatenate(
        parts + tops + highs + lows + [jnp.zeros((2, 128), F32)], axis=0
    ).astype(BF)
    for z in range(Z):
        out[z] = full
    owned = arrived[:, 38, :].astype(F32).astype(BF)
    for t in range(2):
        put = (iota((16, 128), 0) == iota((16, 128), 1) // 8).astype(BF)
        by_lane = dot(owned[t * 16 : (t + 1) * 16], put, ((0,), (0,)))
        mine = iota((128, 128), 0) // B == iota((128, 128), 1) % 8
        by_lane = jnp.where(mine, by_lane, 0.0).reshape(8, B, 128)
        hidden_cols[:, t * 128 : (t + 1) * 128] = jnp.sum(by_lane, axis=0)


def finish_context(arrived, dealt, context, out):
    z = lax.axis_index("z")
    weights = jnp.concatenate(
        [dealt[:, t * 16 : (t + 1) * 16, :].reshape(Z * 16, 128) for t in range(2)], axis=1
    )
    contexts, terms = [], []
    for i in range(2):
        mixed, _, mass = merge(arrived, i)
        done = (mixed / mass).astype(BF)
        mine = (iota((8, 128), 1) == z * 8 + iota((8, 128), 0)).astype(BF)
        contexts.append(dot(mine, done, ((1,), (1,))))
        tile = (iota((16, 256), 0) == iota((16, 256), 1) % 16).astype(BF)
        tiled = dot(done, tile, ((0,), (0,)))
        block = iota((128, 256), 0) // 8 == iota((128, 256), 1) // 16
        tiled = jnp.where(block, tiled, 0.0).astype(BF)
        term = dot(tiled, weights, ((1,), (0,)))
        terms.append(jnp.sum(term.reshape(Z, 8, COLS), axis=0))
    context[...] = jnp.concatenate(contexts, axis=0).astype(BF)
    term = jnp.concatenate(terms, axis=0).astype(BF)
    for k in range(PLANE):
        out[k] = term


def slots(ids, expert, slot):
    hits = jnp.zeros(slot.shape, F32)
    for k in range(8):
        hits += (ids[k : k + 1, :] == expert).astype(F32)
    before = (iota((B, B), 0) < iota((B, B), 1)).astype(BF)
    rank = dot(hits.astype(BF), before, ((1,), (0,)))
    return (hits > 0.5) & (jnp.abs(rank - slot.astype(F32)) < 0.5)


def make_mid(arrived, hidden_cols, expert_ids, out, mid_part):
    x, _, cy = coordinates()
    projected = jnp.sum(arrived[...].astype(F32), axis=0)
    mid = (projected + hidden_cols[...]).astype(BF)
    row = iota((128, B), 0)
    table = slots(expert_ids[...], x * Z + row // 8, row % 4)
    picked = jnp.zeros((128, 128), F32)
    for t in range(2):
        half = (table & (row // 4 % 2 == t)).astype(BF)
        picked += dot(half, mid[:, t * 128 : (t + 1) * 128], ((1,), (0,)))
    out[...] = picked.reshape(Z, 8, 128).astype(BF)
    mine = iota((8, COLS), 1) == x * 64 + cy * 8 + iota((8, COLS), 0)
    mid_part[...] = dot(mine.astype(BF), mid, ((1,), (1,)))


def sort_columns(tiles):
    lane = iota((8, 128), 1)
    for bit in (32, 16, 8):
        low = lane // bit % 2 == 0
        high = lane // (2 * bit) % 2 == 0
        tiles = [
            jnp.where(
                low == high,
                tile,
                jnp.where(high, pltpu.roll(tile, 128 - bit, 1), pltpu.roll(tile, bit, 1)),
            )
            for tile in tiles
        ]
    for step in (4, 2, 1):
        low = lane // (16 * step) % 2 == 0
        swapped = list(tiles)
        for v in range(8):
            if v & step == 0:
                first, second = tiles[v], tiles[v + step]
                swapped[v] = jnp.where(low, first, pltpu.roll(second, 16 * step, 1))
                swapped[v + step] = jnp.where(low, pltpu.roll(first, 128 - 16 * step, 1), second)
        tiles = swapped
    return tiles


def experts(arrived, gain, expert_ids, route_weights, w_gate, w_up, w_down, out):
    x, z, _ = coordinates()
    expert = x * Z + z
    ids = expert_ids[...]
    routes = route_weights[...]
    table = slots(ids, expert, iota((8, B), 0))
    share = routes / jnp.sum(routes, axis=0, keepdims=True)
    weight = jnp.sum(jnp.where(ids == expert, share, 0.0), axis=0, keepdims=True)
    coefficient = jnp.sum(jnp.where(table, weight, 0.0), axis=1, keepdims=True)
    first_half = iota((8, 128), 0) < 4
    gains = gain[...].astype(F32)
    tiles, scaled = [], []
    for p in range(2):
        for v in range(Z // 2):
            tile = halves(arrived[2 * v].astype(F32), arrived[2 * v + 1].astype(F32), p)
            low, high = p * 8 + v, (2 + p) * 8 + v
            tiles.append(tile * tile)
            scaled.append(
                tile * jnp.where(first_half, gains[low : low + 1], gains[high : high + 1])
            )
    squares = sum(tiles[1:], tiles[0])
    squares = squares + jnp.concatenate([squares[4:], squares[:4]], axis=0)
    scale = lax.rsqrt(jnp.sum(squares, axis=1, keepdims=True) * (1.0 / D) + 1e-06)
    picked = jnp.concatenate([(tile * scale).astype(BF) for tile in scaled], axis=1)

    def project(weights):
        near = dot(picked, weights[:, : D // 2], ((1,), (1,)))
        far = dot(picked, weights[:, D // 2 :], ((1,), (1,)))
        return near + jnp.concatenate([far[4:], far[:4]], axis=0)

    gate = project(w_gate)
    upward = project(w_up)
    hidden_units = (gate / (1.0 + jnp.exp(-gate)) * upward).astype(BF)
    weighted = dot(hidden_units, w_down[...], ((1,), (0,))) * coefficient
    for group in range(X):
        start = group * 1024
        tiles = [weighted[:, start + v * 128 : start + (v + 1) * 128] for v in range(8)]
        for c, tile in enumerate(sort_columns(tiles)):
            out[group * CY + c] = tile[:4].astype(BF)


def sum_experts(arrived, expert_ids, out):
    z = lax.axis_index("z")
    parts = [
        jnp.sum(arrived[x * CY : (x + 1) * CY].astype(F32), axis=0) for x in range(X)
    ]
    row = iota((4 * X, B), 0)
    table = slots(expert_ids[...], row // 4 * Z + z, row % 4).astype(F32)
    turned = dot(jnp.concatenate(parts, axis=0), table, ((0,), (0,)), EXACT)
    out[...] = turned.reshape(Z, 8, B).astype(BF)


def finish_layer(arrived, mid_part, context, out, context_out):
    out[...] = (mid_part[...] + jnp.sum(arrived[...].astype(F32), axis=0)).astype(BF)
    context_out[...] = context[...]


def call(body, outs, arrays, far=(), scratch=(), limit=16):
    vmem = pl.BlockSpec(memory_space=pltpu.VMEM)
    remote = pl.BlockSpec(memory_space=pltpu.HBM)
    single = not isinstance(outs, list)
    return pl.pallas_call(
        body,
        out_shape=outs,
        in_specs=[vmem] * len(arrays) + [remote] * len(far),
        out_specs=vmem if single else [vmem] * len(outs),
        scratch_shapes=list(scratch),
        compiler_params=pltpu.CompilerParams(vmem_limit_bytes=limit * 1024 * 1024),
    )(*arrays, *far)


def swap(blocks, axes):
    return lax.all_to_all(blocks, axes, 0, 0, tiled=True)


def shards(
    query,
    key_cache,
    value_cache,
    lengths,
    hidden_in,
    out_proj,
    norm_gain,
    expert_ids,
    route_weights,
    w_gate,
    w_up,
    w_down,
):
    ids, routes = expert_ids.T, route_weights.T
    dma, vmem = pltpu.SemaphoreType.DMA, pltpu.VMEM

    def shape(*dims, dtype=BF):
        return jax.ShapeDtypeStruct(dims, dtype)

    dealt = swap(
        call(
            deal_out,
            shape(Z, 40, 128),
            (),
            (query, out_proj),
            (vmem((B, 16), BF), vmem((16, D), BF), dma((2,))),
            62,
        ),
        "z",
    )
    spread, extra = call(
        spread_query,
        [shape(PLANE, 32, 128), shape(B + 8, 128, dtype=F32)],
        (dealt, lengths.reshape(1, B), hidden_in.T),
    )
    partial = call(
        attend,
        shape(PLANE, 40, 128),
        (swap(spread, PLANE_AXES), key_cache, value_cache, extra),
    )
    merged, hidden_cols = call(
        merge_plane,
        [shape(Z, 40, 128), shape(B, COLS, dtype=F32)],
        (swap(partial, PLANE_AXES),),
    )
    context, term = call(
        finish_context,
        [shape(B, 16), shape(PLANE, B, COLS)],
        (swap(merged, "z"), dealt),
    )
    picked, mid_part = call(
        make_mid,
        [shape(Z, 8, 128), shape(8, B, dtype=F32)],
        (swap(term, PLANE_AXES), hidden_cols, ids),
    )
    mixture = call(
        experts,
        shape(PLANE, 4, 128),
        (swap(picked, "z"), norm_gain.reshape(PLANE, 128), ids, routes, w_gate, w_up, w_down),
    )
    summed = call(sum_experts, shape(Z, 8, B), (swap(mixture, PLANE_AXES), ids))
    layer_out, context = call(
        finish_layer, [shape(8, B), shape(B, 16)], (swap(summed, "z"), mid_part, context)
    )
    return context, layer_out.T


def solution(mesh):
    fine = Mesh(np.asarray(mesh.devices).reshape(X, Z, 2, 4), ALL_AXES)
    columns, rows = P(None, ALL_AXES), P(ALL_AXES, None)
    cache = P(None, ALL_AXES, None)
    placed = (
        columns,
        cache,
        cache,
        P(),
        columns,
        rows,
        P(),
        P(),
        P(),
        rows,
        rows,
        rows,
    )
    return jax.shard_map(
        shards,
        mesh=fine,
        in_specs=placed,
        out_specs=(columns, columns),
        check_vma=False,
    )
```

```python
import math

import jax
import jax.numpy as jnp
import numpy as np
from jax import lax
from jax.experimental import pallas as pl
from jax.experimental.pallas import tpu as pltpu
from jax.sharding import Mesh
from jax.sharding import PartitionSpec as P

HD = 128
X, Z, CY = 4, 16, 8
PLANE = X * CY
B = 16
D = 4096
COLS = D // Z
SPAN = 32
FLOOR = -1e30
BF = jnp.bfloat16
F32 = jnp.float32
PLANE_AXES = ("x", "c", "y")
ALL_AXES = ("x", "z", "c", "y")
EXACT = lax.Precision.HIGHEST


def iota(shape, dimension):
    return lax.broadcasted_iota(jnp.int32, shape, dimension)


def dot(a, b, dims, precision=None):
    return lax.dot_general(
        a, b, (dims, ((), ())), preferred_element_type=F32, precision=precision
    )


def eye(n, dtype=BF):
    return (iota((n, n), 0) == iota((n, n), 1)).astype(dtype)


def halves(first, second, high):
    low_lanes = iota(first.shape, 1) < 64
    if high:
        return jnp.where(low_lanes, pltpu.roll(first, 64, 1), second)
    return jnp.where(low_lanes, first, pltpu.roll(second, 64, 1))


def coordinates():
    x, z = lax.axis_index("x"), lax.axis_index("z")
    return x, z, lax.axis_index("c") * 4 + lax.axis_index("y")


def deal_out(query, out_proj, out, held_query, held, sems):
    copies = [
        pltpu.make_async_copy(query, held_query, sems.at[0]),
        pltpu.make_async_copy(out_proj, held, sems.at[1]),
    ]
    for copy in copies:
        copy.start()
    copies[0].wait()
    own = held_query[...]
    parts = []
    for i in range(2):
        put = (iota((16, 128), 0) + i * 16 == iota((16, 128), 1)).astype(BF)
        parts.append(dot(own, put, ((1,), (0,)))[i * 8 : (i + 1) * 8])
    wide = (parts[0] + parts[1]).astype(BF)
    copies[1].wait()
    for v in range(Z // 2):
        tiles = [
            held[:, x * 1024 + v * 128 : x * 1024 + (v + 1) * 128] for x in range(X)
        ]
        for high in range(2):
            pieces = [halves(tiles[0], tiles[1], high), halves(tiles[2], tiles[3], high), wide]
            out[2 * v + high] = jnp.concatenate(pieces, axis=0)


def spread_query(arrived, lengths, hidden, out, rows_out):
    rows = arrived[:, 32:40, :].astype(F32).reshape(128, 128).astype(BF)
    turned = dot(rows, eye(128), ((0,), (0,)))[:32].astype(BF)
    for k in range(PLANE):
        out[k] = turned
    own = iota((B, B), 0) == iota((B, B), 1)
    column = jnp.sum(jnp.where(own, lengths[...].astype(F32), 0.0), axis=1, keepdims=True)
    rows_out[0:B] = jnp.broadcast_to(column, (B, 128))
    spot = (iota((B, 128), 0) == iota((B, 128), 1) % B).astype(BF)
    repeated = dot(hidden[...], spot, ((1,), (0,)))
    own = jnp.where(iota((8, 128), 0) == iota((8, 128), 1) // B, repeated, 0.0)
    rows_out[B : B + 8] = jnp.broadcast_to(jnp.sum(own, axis=0, keepdims=True), (8, 128))


def attend(gathered, keys, values, extra, out):
    x, z, cy = coordinates()
    device = (x * Z + z) * CY + cy
    lane_j = iota((SPAN, 128), 1) % 8
    position = device * SPAN + iota((SPAN, 128), 0)
    own = extra[B : B + 1]
    zero = jnp.zeros((1, 128), F32)
    position = position.astype(F32)
    limit = extra[0:B]
    valids = []
    for i in range(2):
        rows = [
            (lane_j == j) & (position < limit[i * 8 + j : i * 8 + j + 1]) for j in range(8)
        ]
        valids.append(jnp.concatenate([r.astype(F32) for r in rows], axis=0) > 0.5)
    for g in range(X):
        parts, tops, highs, lows = [], [], [], []
        for i in range(2):
            query = gathered[g * CY : (g + 1) * CY, i * 16 : (i + 1) * 16, :].reshape(HD, 128)
            k = keys[i * 8 : (i + 1) * 8, :, g * HD : (g + 1) * HD].reshape(8 * SPAN, HD)
            v = values[i * 8 : (i + 1) * 8, :, g * HD : (g + 1) * HD].reshape(8 * SPAN, HD)
            scores = dot(k, query, ((1,), (0,))) * (1.0 / math.sqrt(HD))
            scores = jnp.where(valids[i], scores, FLOOR)
            top = jnp.max(scores, axis=0, keepdims=True).astype(BF).astype(F32)
            weights = jnp.where(valids[i], jnp.exp(scores - top), 0.0).astype(BF)
            total = jnp.sum(weights.astype(F32), axis=0, keepdims=True)
            high = total.astype(BF).astype(F32)
            parts.append(dot(v, weights, ((0,), (0,))))
            tops.append(top)
            highs.append(high)
            lows.append(total - high)
        block = jnp.concatenate(tops + highs + lows + [own, zero], axis=0)
        for c in range(CY):
            pieces = [part[c * 16 : (c + 1) * 16] for part in parts]
            out[g * CY + c] = jnp.concatenate(pieces + [block], axis=0).astype(BF)


def merge(arrived, i):
    top = arrived[:, 32 + i, :].astype(F32)
    total = arrived[:, 34 + i, :].astype(F32) + arrived[:, 36 + i, :].astype(F32)
    best = jnp.max(top, axis=0, keepdims=True)
    scale = jnp.exp(top - best)
    mass = jnp.sum(total * scale, axis=0, keepdims=True)
    mixed = arrived[:, i * 16 : (i + 1) * 16, :].astype(F32)
    return jnp.sum(mixed * scale[:, None, :], axis=0), best, mass


def merge_plane(arrived, out, hidden_cols):
    parts, tops, highs, lows = [], [], [], []
    for i in range(2):
        mixed, best, mass = merge(arrived, i)
        high = mass.astype(BF).astype(F32)
        parts.append(mixed)
        tops.append(best)
        highs.append(high)
        lows.append(mass - high)
    full = jnp.concatenate(
        parts + tops + highs + lows + [jnp.zeros((2, 128), F32)], axis=0
    ).astype(BF)
    for z in range(Z):
        out[z] = full
    owned = arrived[:, 38, :].astype(F32).astype(BF)
    for t in range(2):
        put = (iota((16, 128), 0) == iota((16, 128), 1) // 8).astype(BF)
        by_lane = dot(owned[t * 16 : (t + 1) * 16], put, ((0,), (0,)))
        mine = iota((128, 128), 0) // B == iota((128, 128), 1) % 8
        by_lane = jnp.where(mine, by_lane, 0.0).reshape(8, B, 128)
        hidden_cols[:, t * 128 : (t + 1) * 128] = jnp.sum(by_lane, axis=0)


def finish_context(arrived, dealt, context, out):
    z = lax.axis_index("z")
    weights = jnp.concatenate(
        [dealt[:, t * 16 : (t + 1) * 16, :].reshape(Z * 16, 128) for t in range(2)], axis=1
    )
    contexts, terms = [], []
    for i in range(2):
        mixed, _, mass = merge(arrived, i)
        done = (mixed / mass).astype(BF)
        mine = (iota((8, 128), 1) == z * 8 + iota((8, 128), 0)).astype(BF)
        contexts.append(dot(mine, done, ((1,), (1,))))
        tile = (iota((16, 256), 0) == iota((16, 256), 1) % 16).astype(BF)
        tiled = dot(done, tile, ((0,), (0,)))
        block = iota((128, 256), 0) // 8 == iota((128, 256), 1) // 16
        tiled = jnp.where(block, tiled, 0.0).astype(BF)
        term = dot(tiled, weights, ((1,), (0,)))
        terms.append(jnp.sum(term.reshape(Z, 8, COLS), axis=0))
    context[...] = jnp.concatenate(contexts, axis=0).astype(BF)
    term = jnp.concatenate(terms, axis=0).astype(BF)
    for k in range(PLANE):
        out[k] = term


def slots(ids, expert, slot):
    hits = jnp.zeros(slot.shape, F32)
    for k in range(8):
        hits += (ids[k : k + 1, :] == expert).astype(F32)
    before = (iota((B, B), 0) < iota((B, B), 1)).astype(BF)
    rank = dot(hits.astype(BF), before, ((1,), (0,)))
    return (hits > 0.5) & (jnp.abs(rank - slot.astype(F32)) < 0.5)


def make_mid(arrived, hidden_cols, expert_ids, out, mid_part):
    x, _, cy = coordinates()
    projected = jnp.sum(arrived[...].astype(F32), axis=0)
    mid = (projected + hidden_cols[...]).astype(BF)
    row = iota((128, B), 0)
    table = slots(expert_ids[...], x * Z + row // 8, row % 4)
    picked = jnp.zeros((128, 128), F32)
    for t in range(2):
        half = (table & (row // 4 % 2 == t)).astype(BF)
        picked += dot(half, mid[:, t * 128 : (t + 1) * 128], ((1,), (0,)))
    out[...] = picked.reshape(Z, 8, 128).astype(BF)
    mine = iota((8, COLS), 1) == x * 64 + cy * 8 + iota((8, COLS), 0)
    mid_part[...] = dot(mine.astype(BF), mid, ((1,), (1,)))


def sort_columns(tiles):
    lane = iota((8, 128), 1)
    for bit in (32, 16, 8):
        low = lane // bit % 2 == 0
        high = lane // (2 * bit) % 2 == 0
        tiles = [
            jnp.where(
                low == high,
                tile,
                jnp.where(high, pltpu.roll(tile, 128 - bit, 1), pltpu.roll(tile, bit, 1)),
            )
            for tile in tiles
        ]
    for step in (4, 2, 1):
        low = lane // (16 * step) % 2 == 0
        swapped = list(tiles)
        for v in range(8):
            if v & step == 0:
                first, second = tiles[v], tiles[v + step]
                swapped[v] = jnp.where(low, first, pltpu.roll(second, 16 * step, 1))
                swapped[v + step] = jnp.where(low, pltpu.roll(first, 128 - 16 * step, 1), second)
        tiles = swapped
    return tiles


def experts(arrived, gain, expert_ids, route_weights, w_gate, w_up, w_down, out):
    x, z, _ = coordinates()
    expert = x * Z + z
    ids = expert_ids[...]
    routes = route_weights[...]
    table = slots(ids, expert, iota((8, B), 0))
    share = routes / jnp.sum(routes, axis=0, keepdims=True)
    weight = jnp.sum(jnp.where(ids == expert, share, 0.0), axis=0, keepdims=True)
    coefficient = jnp.sum(jnp.where(table, weight, 0.0), axis=1, keepdims=True)
    first_half = iota((8, 128), 0) < 4
    gains = gain[...].astype(F32)
    tiles, scaled = [], []
    for p in range(2):
        for v in range(Z // 2):
            tile = halves(arrived[2 * v].astype(F32), arrived[2 * v + 1].astype(F32), p)
            low, high = p * 8 + v, (2 + p) * 8 + v
            tiles.append(tile * tile)
            scaled.append(
                tile * jnp.where(first_half, gains[low : low + 1], gains[high : high + 1])
            )
    squares = sum(tiles[1:], tiles[0])
    squares = squares + jnp.concatenate([squares[4:], squares[:4]], axis=0)
    scale = lax.rsqrt(jnp.sum(squares, axis=1, keepdims=True) * (1.0 / D) + 1e-06)
    picked = jnp.concatenate([(tile * scale).astype(BF) for tile in scaled], axis=1)

    def project(weights):
        near = dot(picked, weights[:, : D // 2], ((1,), (1,)))
        far = dot(picked, weights[:, D // 2 :], ((1,), (1,)))
        return near + jnp.concatenate([far[4:], far[:4]], axis=0)

    gate = project(w_gate)
    upward = project(w_up)
    hidden_units = (gate / (1.0 + jnp.exp(-gate)) * upward).astype(BF)
    weighted = dot(hidden_units, w_down[...], ((1,), (0,))) * coefficient
    for group in range(X):
        start = group * 1024
        tiles = [weighted[:, start + v * 128 : start + (v + 1) * 128] for v in range(8)]
        for c, tile in enumerate(sort_columns(tiles)):
            out[group * CY + c] = tile[:4].astype(BF)


def sum_experts(arrived, expert_ids, out):
    z = lax.axis_index("z")
    parts = [
        jnp.sum(arrived[x * CY : (x + 1) * CY].astype(F32), axis=0) for x in range(X)
    ]
    row = iota((4 * X, B), 0)
    table = slots(expert_ids[...], row // 4 * Z + z, row % 4).astype(F32)
    turned = dot(jnp.concatenate(parts, axis=0), table, ((0,), (0,)), EXACT)
    out[...] = turned.reshape(Z, 8, B).astype(BF)


def finish_layer(arrived, mid_part, context, out, context_out):
    out[...] = (mid_part[...] + jnp.sum(arrived[...].astype(F32), axis=0)).astype(BF)
    context_out[...] = context[...]


def call(body, outs, arrays, far=(), scratch=(), limit=16):
    vmem = pl.BlockSpec(memory_space=pltpu.VMEM)
    remote = pl.BlockSpec(memory_space=pltpu.HBM)
    single = not isinstance(outs, list)
    return pl.pallas_call(
        body,
        out_shape=outs,
        in_specs=[vmem] * len(arrays) + [remote] * len(far),
        out_specs=vmem if single else [vmem] * len(outs),
        scratch_shapes=list(scratch),
        compiler_params=pltpu.CompilerParams(vmem_limit_bytes=limit * 1024 * 1024),
    )(*arrays, *far)


def swap(blocks, axes):
    return lax.all_to_all(blocks, axes, 0, 0, tiled=True)


def shards(
    query,
    key_cache,
    value_cache,
    lengths,
    hidden_in,
    out_proj,
    norm_gain,
    expert_ids,
    route_weights,
    w_gate,
    w_up,
    w_down,
):
    ids, routes = expert_ids.T, route_weights.T
    dma, vmem = pltpu.SemaphoreType.DMA, pltpu.VMEM

    def shape(*dims, dtype=BF):
        return jax.ShapeDtypeStruct(dims, dtype)

    dealt = swap(
        call(
            deal_out,
            vmem((Z, 40, 128), BF),
            (),
            (query, out_proj),
            (vmem((B, 16), BF), vmem((16, D), BF), dma((2,))),
            62,
        ),
        "z",
    )
    spread, extra = call(
        spread_query,
        [shape(PLANE, 32, 128), shape(B + 8, 128, dtype=F32)],
        (dealt, lengths.reshape(1, B), hidden_in.T),
    )
    partial = call(
        attend,
        shape(PLANE, 40, 128),
        (swap(spread, PLANE_AXES), key_cache, value_cache, extra),
    )
    merged, hidden_cols = call(
        merge_plane,
        [shape(Z, 40, 128), shape(B, COLS, dtype=F32)],
        (swap(partial, PLANE_AXES),),
    )
    context, term = call(
        finish_context,
        [shape(B, 16), shape(PLANE, B, COLS)],
        (swap(merged, "z"), dealt),
    )
    picked, mid_part = call(
        make_mid,
        [shape(Z, 8, 128), shape(8, B, dtype=F32)],
        (swap(term, PLANE_AXES), hidden_cols, ids),
    )
    mixture = call(
        experts,
        shape(PLANE, 4, 128),
        (swap(picked, "z"), norm_gain.reshape(PLANE, 128), ids, routes, w_gate, w_up, w_down),
    )
    summed = call(sum_experts, shape(Z, 8, B), (swap(mixture, PLANE_AXES), ids))
    layer_out, context = call(
        finish_layer, [shape(8, B), shape(B, 16)], (swap(summed, "z"), mid_part, context)
    )
    return context, layer_out.T


def solution(mesh):
    fine = Mesh(np.asarray(mesh.devices).reshape(X, Z, 2, 4), ALL_AXES)
    columns, rows = P(None, ALL_AXES), P(ALL_AXES, None)
    cache = P(None, ALL_AXES, None)
    placed = (
        columns,
        cache,
        cache,
        P(),
        columns,
        rows,
        P(),
        P(),
        P(),
        rows,
        rows,
        rows,
    )
    return jax.shard_map(
        shards,
        mesh=fine,
        in_specs=placed,
        out_specs=(columns, columns),
        check_vma=False,
    )
```

```python
import math

import jax
import jax.numpy as jnp
import numpy as np
from jax import lax
from jax.experimental import pallas as pl
from jax.experimental.pallas import tpu as pltpu
from jax.sharding import Mesh
from jax.sharding import PartitionSpec as P

HD = 128
X, Z, CY = 4, 16, 8
PLANE = X * CY
B = 16
D = 4096
COLS = D // Z
SPAN = 32
FLOOR = -1e30
BF = jnp.bfloat16
F32 = jnp.float32
PLANE_AXES = ("x", "c", "y")
ALL_AXES = ("x", "z", "c", "y")
EXACT = lax.Precision.HIGHEST


def iota(shape, dimension):
    return lax.broadcasted_iota(jnp.int32, shape, dimension)


def dot(a, b, dims, precision=None):
    return lax.dot_general(
        a, b, (dims, ((), ())), preferred_element_type=F32, precision=precision
    )


def eye(n, dtype=BF):
    return (iota((n, n), 0) == iota((n, n), 1)).astype(dtype)


def halves(first, second, high):
    low_lanes = iota(first.shape, 1) < 64
    if high:
        return jnp.where(low_lanes, pltpu.roll(first, 64, 1), second)
    return jnp.where(low_lanes, first, pltpu.roll(second, 64, 1))


def coordinates():
    x, z = lax.axis_index("x"), lax.axis_index("z")
    return x, z, lax.axis_index("c") * 4 + lax.axis_index("y")


def deal_out(query, out_proj, out, held_query, held, sems):
    copies = [pltpu.make_async_copy(query, held_query, sems.at[0])]
    for x in range(X):
        part = pl.ds(x * 1024, 1024)
        copies.append(
            pltpu.make_async_copy(out_proj.at[:, part], held.at[:, part], sems.at[1 + x])
        )
    for copy in copies:
        copy.start()
    copies[0].wait()
    own = held_query[...]
    parts = []
    for i in range(2):
        put = (iota((16, 128), 0) + i * 16 == iota((16, 128), 1)).astype(BF)
        parts.append(dot(own, put, ((1,), (0,)))[i * 8 : (i + 1) * 8])
    wide = (parts[0] + parts[1]).astype(BF)
    for copy in copies[1:]:
        copy.wait()
    for v in range(Z // 2):
        tiles = [
            held[:, x * 1024 + v * 128 : x * 1024 + (v + 1) * 128] for x in range(X)
        ]
        for high in range(2):
            pieces = [halves(tiles[0], tiles[1], high), halves(tiles[2], tiles[3], high), wide]
            out[2 * v + high] = jnp.concatenate(pieces, axis=0)


def spread_query(arrived, lengths, hidden, out, rows_out):
    rows = arrived[:, 32:40, :].astype(F32).reshape(128, 128).astype(BF)
    turned = dot(rows, eye(128), ((0,), (0,)))[:32].astype(BF)
    for k in range(PLANE):
        out[k] = turned
    own = iota((B, B), 0) == iota((B, B), 1)
    column = jnp.sum(jnp.where(own, lengths[...].astype(F32), 0.0), axis=1, keepdims=True)
    rows_out[0:B] = jnp.broadcast_to(column, (B, 128))
    spot = (iota((B, 128), 0) == iota((B, 128), 1) % B).astype(BF)
    repeated = dot(hidden[...], spot, ((1,), (0,)))
    own = jnp.where(iota((8, 128), 0) == iota((8, 128), 1) // B, repeated, 0.0)
    rows_out[B : B + 8] = jnp.broadcast_to(jnp.sum(own, axis=0, keepdims=True), (8, 128))


def attend(gathered, keys, values, extra, out):
    x, z, cy = coordinates()
    device = (x * Z + z) * CY + cy
    lane_j = iota((SPAN, 128), 1) % 8
    position = device * SPAN + iota((SPAN, 128), 0)
    own = extra[B : B + 1]
    zero = jnp.zeros((1, 128), F32)
    position = position.astype(F32)
    limit = extra[0:B]
    valids = []
    for i in range(2):
        rows = [
            (lane_j == j) & (position < limit[i * 8 + j : i * 8 + j + 1]) for j in range(8)
        ]
        valids.append(jnp.concatenate([r.astype(F32) for r in rows], axis=0) > 0.5)
    for g in range(X):
        parts, tops, highs, lows = [], [], [], []
        for i in range(2):
            query = gathered[g * CY : (g + 1) * CY, i * 16 : (i + 1) * 16, :].reshape(HD, 128)
            k = keys[i * 8 : (i + 1) * 8, :, g * HD : (g + 1) * HD].reshape(8 * SPAN, HD)
            v = values[i * 8 : (i + 1) * 8, :, g * HD : (g + 1) * HD].reshape(8 * SPAN, HD)
            scores = dot(k, query, ((1,), (0,))) * (1.0 / math.sqrt(HD))
            scores = jnp.where(valids[i], scores, FLOOR)
            top = jnp.max(scores, axis=0, keepdims=True).astype(BF).astype(F32)
            weights = jnp.where(valids[i], jnp.exp(scores - top), 0.0).astype(BF)
            total = jnp.sum(weights.astype(F32), axis=0, keepdims=True)
            high = total.astype(BF).astype(F32)
            parts.append(dot(v, weights, ((0,), (0,))))
            tops.append(top)
            highs.append(high)
            lows.append(total - high)
        block = jnp.concatenate(tops + highs + lows + [own, zero], axis=0)
        for c in range(CY):
            pieces = [part[c * 16 : (c + 1) * 16] for part in parts]
            out[g * CY + c] = jnp.concatenate(pieces + [block], axis=0).astype(BF)


def merge(arrived, i):
    top = arrived[:, 32 + i, :].astype(F32)
    total = arrived[:, 34 + i, :].astype(F32) + arrived[:, 36 + i, :].astype(F32)
    best = jnp.max(top, axis=0, keepdims=True)
    scale = jnp.exp(top - best)
    mass = jnp.sum(total * scale, axis=0, keepdims=True)
    mixed = arrived[:, i * 16 : (i + 1) * 16, :].astype(F32)
    return jnp.sum(mixed * scale[:, None, :], axis=0), best, mass


def merge_plane(arrived, out, hidden_cols):
    parts, tops, highs, lows = [], [], [], []
    for i in range(2):
        mixed, best, mass = merge(arrived, i)
        high = mass.astype(BF).astype(F32)
        parts.append(mixed)
        tops.append(best)
        highs.append(high)
        lows.append(mass - high)
    full = jnp.concatenate(
        parts + tops + highs + lows + [jnp.zeros((2, 128), F32)], axis=0
    ).astype(BF)
    for z in range(Z):
        out[z] = full
    owned = arrived[:, 38, :].astype(F32).astype(BF)
    for t in range(2):
        put = (iota((16, 128), 0) == iota((16, 128), 1) // 8).astype(BF)
        by_lane = dot(owned[t * 16 : (t + 1) * 16], put, ((0,), (0,)))
        mine = iota((128, 128), 0) // B == iota((128, 128), 1) % 8
        by_lane = jnp.where(mine, by_lane, 0.0).reshape(8, B, 128)
        hidden_cols[:, t * 128 : (t + 1) * 128] = jnp.sum(by_lane, axis=0)


def finish_context(arrived, dealt, context, out):
    z = lax.axis_index("z")
    weights = jnp.concatenate(
        [dealt[:, t * 16 : (t + 1) * 16, :].reshape(Z * 16, 128) for t in range(2)], axis=1
    )
    contexts, terms = [], []
    for i in range(2):
        mixed, _, mass = merge(arrived, i)
        done = (mixed / mass).astype(BF)
        mine = (iota((8, 128), 1) == z * 8 + iota((8, 128), 0)).astype(BF)
        contexts.append(dot(mine, done, ((1,), (1,))))
        tile = (iota((16, 256), 0) == iota((16, 256), 1) % 16).astype(BF)
        tiled = dot(done, tile, ((0,), (0,)))
        block = iota((128, 256), 0) // 8 == iota((128, 256), 1) // 16
        tiled = jnp.where(block, tiled, 0.0).astype(BF)
        term = dot(tiled, weights, ((1,), (0,)))
        terms.append(jnp.sum(term.reshape(Z, 8, COLS), axis=0))
    context[...] = jnp.concatenate(contexts, axis=0).astype(BF)
    term = jnp.concatenate(terms, axis=0).astype(BF)
    for k in range(PLANE):
        out[k] = term


def slots(ids, expert, slot):
    hits = jnp.zeros(slot.shape, F32)
    for k in range(8):
        hits += (ids[k : k + 1, :] == expert).astype(F32)
    before = (iota((B, B), 0) < iota((B, B), 1)).astype(BF)
    rank = dot(hits.astype(BF), before, ((1,), (0,)))
    return (hits > 0.5) & (jnp.abs(rank - slot.astype(F32)) < 0.5)


def make_mid(arrived, hidden_cols, expert_ids, out, mid_part):
    x, _, cy = coordinates()
    projected = jnp.sum(arrived[...].astype(F32), axis=0)
    mid = (projected + hidden_cols[...]).astype(BF)
    row = iota((128, B), 0)
    table = slots(expert_ids[...], x * Z + row // 8, row % 4)
    picked = jnp.zeros((128, 128), F32)
    for t in range(2):
        half = (table & (row // 4 % 2 == t)).astype(BF)
        picked += dot(half, mid[:, t * 128 : (t + 1) * 128], ((1,), (0,)))
    out[...] = picked.reshape(Z, 8, 128).astype(BF)
    mine = iota((8, COLS), 1) == x * 64 + cy * 8 + iota((8, COLS), 0)
    mid_part[...] = dot(mine.astype(BF), mid, ((1,), (1,)))


def sort_columns(tiles):
    lane = iota((8, 128), 1)
    for bit in (32, 16, 8):
        low = lane // bit % 2 == 0
        high = lane // (2 * bit) % 2 == 0
        tiles = [
            jnp.where(
                low == high,
                tile,
                jnp.where(high, pltpu.roll(tile, 128 - bit, 1), pltpu.roll(tile, bit, 1)),
            )
            for tile in tiles
        ]
    for step in (4, 2, 1):
        low = lane // (16 * step) % 2 == 0
        swapped = list(tiles)
        for v in range(8):
            if v & step == 0:
                first, second = tiles[v], tiles[v + step]
                swapped[v] = jnp.where(low, first, pltpu.roll(second, 16 * step, 1))
                swapped[v + step] = jnp.where(low, pltpu.roll(first, 128 - 16 * step, 1), second)
        tiles = swapped
    return tiles


def experts(arrived, gain, expert_ids, route_weights, w_gate, w_up, w_down, out):
    x, z, _ = coordinates()
    expert = x * Z + z
    ids = expert_ids[...]
    routes = route_weights[...]
    table = slots(ids, expert, iota((8, B), 0))
    share = routes / jnp.sum(routes, axis=0, keepdims=True)
    weight = jnp.sum(jnp.where(ids == expert, share, 0.0), axis=0, keepdims=True)
    coefficient = jnp.sum(jnp.where(table, weight, 0.0), axis=1, keepdims=True)
    first_half = iota((8, 128), 0) < 4
    gains = gain[...].astype(F32)
    tiles, scaled = [], []
    for p in range(2):
        for v in range(Z // 2):
            tile = halves(arrived[2 * v].astype(F32), arrived[2 * v + 1].astype(F32), p)
            low, high = p * 8 + v, (2 + p) * 8 + v
            tiles.append(tile * tile)
            scaled.append(
                tile * jnp.where(first_half, gains[low : low + 1], gains[high : high + 1])
            )
    squares = sum(tiles[1:], tiles[0])
    squares = squares + jnp.concatenate([squares[4:], squares[:4]], axis=0)
    scale = lax.rsqrt(jnp.sum(squares, axis=1, keepdims=True) * (1.0 / D) + 1e-06)
    picked = jnp.concatenate([(tile * scale).astype(BF) for tile in scaled], axis=1)

    def project(weights):
        near = dot(picked, weights[:, : D // 2], ((1,), (1,)))
        far = dot(picked, weights[:, D // 2 :], ((1,), (1,)))
        return near + jnp.concatenate([far[4:], far[:4]], axis=0)

    gate = project(w_gate)
    upward = project(w_up)
    hidden_units = (gate / (1.0 + jnp.exp(-gate)) * upward).astype(BF)
    weighted = dot(hidden_units, w_down[...], ((1,), (0,))) * coefficient
    for group in range(X):
        start = group * 1024
        tiles = [weighted[:, start + v * 128 : start + (v + 1) * 128] for v in range(8)]
        for c, tile in enumerate(sort_columns(tiles)):
            out[group * CY + c] = tile[:4].astype(BF)


def sum_experts(arrived, expert_ids, out):
    z = lax.axis_index("z")
    parts = [
        jnp.sum(arrived[x * CY : (x + 1) * CY].astype(F32), axis=0) for x in range(X)
    ]
    row = iota((4 * X, B), 0)
    table = slots(expert_ids[...], row // 4 * Z + z, row % 4).astype(F32)
    turned = dot(jnp.concatenate(parts, axis=0), table, ((0,), (0,)), EXACT)
    out[...] = turned.reshape(Z, 8, B).astype(BF)


def finish_layer(arrived, mid_part, context, out, context_out):
    out[...] = (mid_part[...] + jnp.sum(arrived[...].astype(F32), axis=0)).astype(BF)
    context_out[...] = context[...]


def call(body, outs, arrays, far=(), scratch=(), limit=16):
    vmem = pl.BlockSpec(memory_space=pltpu.VMEM)
    remote = pl.BlockSpec(memory_space=pltpu.HBM)
    single = not isinstance(outs, list)
    return pl.pallas_call(
        body,
        out_shape=outs,
        in_specs=[vmem] * len(arrays) + [remote] * len(far),
        out_specs=vmem if single else [vmem] * len(outs),
        scratch_shapes=list(scratch),
        compiler_params=pltpu.CompilerParams(vmem_limit_bytes=limit * 1024 * 1024),
    )(*arrays, *far)


def swap(blocks, axes):
    return lax.all_to_all(blocks, axes, 0, 0, tiled=True)


def shards(
    query,
    key_cache,
    value_cache,
    lengths,
    hidden_in,
    out_proj,
    norm_gain,
    expert_ids,
    route_weights,
    w_gate,
    w_up,
    w_down,
):
    ids, routes = expert_ids.T, route_weights.T
    dma, vmem = pltpu.SemaphoreType.DMA, pltpu.VMEM

    def shape(*dims, dtype=BF):
        return jax.ShapeDtypeStruct(dims, dtype)

    dealt = swap(
        call(
            deal_out,
            vmem((Z, 40, 128), BF),
            (),
            (query, out_proj),
            (vmem((B, 16), BF), vmem((16, D), BF), dma((1 + X,))),
            62,
        ),
        "z",
    )
    spread, extra = call(
        spread_query,
        [shape(PLANE, 32, 128), shape(B + 8, 128, dtype=F32)],
        (dealt, lengths.reshape(1, B), hidden_in.T),
    )
    partial = call(
        attend,
        shape(PLANE, 40, 128),
        (swap(spread, PLANE_AXES), key_cache, value_cache, extra),
    )
    merged, hidden_cols = call(
        merge_plane,
        [shape(Z, 40, 128), shape(B, COLS, dtype=F32)],
        (swap(partial, PLANE_AXES),),
    )
    context, term = call(
        finish_context,
        [shape(B, 16), shape(PLANE, B, COLS)],
        (swap(merged, "z"), dealt),
    )
    picked, mid_part = call(
        make_mid,
        [shape(Z, 8, 128), shape(8, B, dtype=F32)],
        (swap(term, PLANE_AXES), hidden_cols, ids),
    )
    mixture = call(
        experts,
        shape(PLANE, 4, 128),
        (swap(picked, "z"), norm_gain.reshape(PLANE, 128), ids, routes, w_gate, w_up, w_down),
    )
    summed = call(sum_experts, shape(Z, 8, B), (swap(mixture, PLANE_AXES), ids))
    layer_out, context = call(
        finish_layer, [shape(8, B), shape(B, 16)], (swap(summed, "z"), mid_part, context)
    )
    return context, layer_out.T


def solution(mesh):
    fine = Mesh(np.asarray(mesh.devices).reshape(X, Z, 2, 4), ALL_AXES)
    columns, rows = P(None, ALL_AXES), P(ALL_AXES, None)
    cache = P(None, ALL_AXES, None)
    placed = (
        columns,
        cache,
        cache,
        P(),
        columns,
        rows,
        P(),
        P(),
        P(),
        rows,
        rows,
        rows,
    )
    return jax.shard_map(
        shards,
        mesh=fine,
        in_specs=placed,
        out_specs=(columns, columns),
        check_vma=False,
    )
```
